512 devices in a mesh: band: 8 (over z), tile: 64 (over x, y, core).
Axes of the slice: x: 4, y: 8, z: 8, core: 2. Of those that a mesh axis runs over, the one named last changes fastest.
Arguments:
- frames: bfloat16 [512, 256, 512], P('tile', 'band'), may hold values from -6 to 6
- disk_mask: int32 [256, 512], P('band'), may hold values from 0 to 1, as said below
- offsets: int32 [8, 8, 2], replicated, may hold values from -4 to 4, as said below
- filter_gain: float32 [128], replicated, may hold values from 0.5 to 2
- filter_mix: float32 [128], replicated, may hold values from -1 to 1
Outputs:
- cross_spectra: float32 [64, 128, 8, 2, 128], P('band', 'tile')
The draws below stay inside these ranges and needn't reach their ends.
Inputs may be any that keep to these rules, and one draw needn't show every extreme that they name: `disk_mask`: 1 on the pixels of one disk whose centre lies within the image rows, 0 elsewhere; the first column is off the disk. In every distance's list the row offsets and the column offsets each reach -4 and 4.
All inputs are finite; a program needn't handle non-finite values.
Results may differ from the reference program's by a relative error of at most 0.006.
Values may be sent and summed in bfloat16 or wider, within the bound.
No kernel may reach another device: no remote copies, remote signals or barrier semaphores. Data moves between devices by JAX's collectives and lax.ppermute only.
A program may use at most 128 MiB of HBM per device.

```python
import math
import jax
import jax.numpy as jnp
from jax import lax

FRAMES = 512
FREQ = 128
DIST = 8
OFFS = 8
FLO = 48
RAD = 4
MARGIN = 5
NR = 256
NC = 512


def draw_disk_mask(key, part):
    key = jax.random.fold_in(key, 11)
    first, second, third = jax.random.split(key, 3)
    centre_row = jax.random.randint(first, (), 0, NR)
    centre_col = jax.random.randint(second, (), NC // 2 - NC // 16, NC // 2 + NC // 16 + 1)
    radius = jax.random.randint(third, (), NC * 3 // 8, NC * 7 // 16)
    row_index = jnp.arange(NR, dtype=jnp.int32)[:, None] - centre_row
    col_index = jnp.arange(NC, dtype=jnp.int32)[None, :] - centre_col
    inside = row_index * row_index + col_index * col_index <= radius * radius
    return inside.astype(jnp.int32)


def draw_offsets(key, part):
    key = jax.random.fold_in(key, 23)
    values = jax.random.randint(key, (DIST, OFFS, 2), -RAD, RAD + 1)
    values = values.at[:, 0, 0].set(RAD).at[:, 1, 0].set(-RAD)
    values = values.at[:, 2, 1].set(RAD).at[:, 3, 1].set(-RAD)
    return values.astype(jnp.int32)


def shard_levels(key, extent, cuts, low, top_value):
    loudness, own = 1.0, jax.random.fold_in(key, 6)
    for axis_at, parts in cuts:
        steps = jnp.exp(jax.random.uniform(jax.random.fold_in(own, axis_at), (parts,), jnp.float32, low / len(cuts), top_value / len(cuts)))
        loudness = loudness * jnp.repeat(steps, extent[axis_at] // parts).reshape([-1 if axis == axis_at else 1 for axis in range(len(extent))])
    return loudness


def centred(stream_key, extent, deviation, reach, cuts=(), kind=jnp.bfloat16):
    result = jax.random.normal(stream_key, extent, jnp.float32) * deviation
    if len(cuts) > 0:
        result = shard_levels(stream_key, extent, cuts, -0.22, 0.18) * result
    return jnp.clip(result, min=-reach, max=reach).astype(kind)


def setup_inputs(seed: int = 0) -> dict:
    keys = jax.random.split(jax.random.key(seed), 6)
    return {
        "frames": centred(keys[0], (FRAMES, NR, NC), 1.0, 6.0, ((0, 64), (1, 8))),
        "disk_mask": draw_disk_mask(jax.random.fold_in(keys[5], 71), 0),
        "offsets": draw_offsets(jax.random.fold_in(keys[5], 71), 0),
        "filter_gain": jnp.clip(jnp.exp(jax.random.uniform(keys[3], (FREQ,), jnp.float32, math.log(0.5), math.log(2.0))), 0.5, 2.0),
        "filter_mix": jnp.clip(jax.random.uniform(keys[4], (FREQ,), jnp.float32, -1.0, 1.0), -1.0, 1.0),
    }


def dft_table():
    times = jnp.arange(FRAMES, dtype=jnp.int32)
    freqs = FLO + jnp.arange(FREQ, dtype=jnp.int32)
    phases = times[:, None] * freqs[None, :] % FRAMES
    angles = phases.astype(jnp.float32) * (2.0 * math.pi / FRAMES)
    factor = 1.0 / math.sqrt(FRAMES)
    return jnp.concatenate([jnp.cos(angles) * factor, -jnp.sin(angles) * factor], axis=1).astype(jnp.bfloat16)

def cross_blocks(centre, annulus, weight, denom):
    real_c = centre[..., :FREQ]
    imag_c = centre[..., FREQ:]
    real_a = annulus[..., :FREQ]
    imag_a = annulus[..., FREQ:]
    cross = jnp.stack([real_c * real_a + imag_c * imag_a, real_c * imag_a - imag_c * real_a], axis=2)
    cross = cross * weight[:, :, None, None]
    row_count = weight.shape[0]
    col_count = weight.shape[1]
    summed = cross.reshape(row_count // 4, 4, col_count // 4, 4, 2, FREQ).sum(axis=(1, 3))
    return summed / denom[:, :, None, None]

def reference(frames, disk_mask, offsets, filter_gain, filter_mix):
    masked = frames * disk_mask[None].astype(jnp.bfloat16)
    flat_series = masked.reshape(FRAMES, NR * NC)
    spectrum = lax.dot_general(flat_series, dft_table(), (((0,), (0,)), ((), ())), preferred_element_type=jnp.float32)
    spectrum = spectrum.astype(jnp.bfloat16).reshape(NR, NC, 2 * FREQ)
    padded = jnp.pad(spectrum.astype(jnp.float32), ((MARGIN, MARGIN), (MARGIN, MARGIN), (0, 0)))
    inner = padded[1:-1, 1:-1]
    beside_all = 0.25 * (padded[2:, 1:-1] + padded[:-2, 1:-1] + padded[1:-1, 2:] + padded[1:-1, :-2])
    gain_both = jnp.concatenate([filter_gain, filter_gain])
    mix_both = jnp.concatenate([filter_mix, filter_mix])
    filtered = gain_both * inner + mix_both * (beside_all - inner)
    centre = filtered[RAD:RAD + NR, RAD:RAD + NC]
    weight = disk_mask.astype(jnp.float32)
    counts = weight.reshape(NR // 4, 4, NC // 4, 4).sum(axis=(1, 3))
    denom = jnp.maximum(counts, 1.0)
    blocks_all = []
    for distance in range(DIST):
        annulus = jnp.zeros((NR, NC, 2 * FREQ), jnp.float32)
        for member in range(OFFS):
            start_row = (RAD + offsets[distance, member, 0]).astype(jnp.int32)
            start_col = (RAD + offsets[distance, member, 1]).astype(jnp.int32)
            annulus = annulus + lax.dynamic_slice(filtered, (start_row, start_col, jnp.int32(0)), (NR, NC, 2 * FREQ))
        blocks_all.append(cross_blocks(centre, annulus, weight, denom))
    return jnp.stack(blocks_all, axis=2)
```

```python
import math

import jax
import jax.numpy as jnp
import numpy as np
from jax import lax
from jax.experimental import pallas as pl
from jax.experimental.pallas import tpu as pltpu
from jax.sharding import PartitionSpec as P

FRAMES = 512
FREQ = 128
DIST = 8
OFFS = 8
FLO = 48
TILES = 64
LOCAL = 8
ROWS = 32
COLS = 8
WIDE = 20
LEAD = 6
BLOCKS = 72
TALL = 48
REACH = 40
SIDE = 16

F32 = jnp.float32
BF16 = jnp.bfloat16


def dft_table():
    times = np.arange(FRAMES, dtype=np.int32)
    freqs = FLO + np.arange(FREQ, dtype=np.int32)
    phases = times[:, None] * freqs[None, :] % FRAMES
    angles = phases.astype(np.float32) * np.float32(2.0 * math.pi / FRAMES)
    factor = np.float32(1.0 / math.sqrt(FRAMES))
    both = np.concatenate([np.cos(angles) * factor, -np.sin(angles) * factor], axis=1)
    return jnp.asarray(both.astype(np.float32)).astype(BF16)


def pack_kernel(frames_ref, mask_ref, out_ref, low_ref, high_ref):
    mask = mask_ref[...].astype(F32)
    masked = (frames_ref[...].astype(F32) * mask[None]).astype(BF16)
    flat = masked.reshape(LOCAL * ROWS, mask.shape[1])
    cols = lax.broadcasted_iota(jnp.int32, (BLOCKS, mask.shape[1]), 1)
    block = lax.broadcasted_iota(jnp.int32, (BLOCKS, mask.shape[1]), 0)
    place = cols - 8 * block + LEAD
    rolled = []
    for c in range(COLS):
        pick = jnp.where(place == c, 1.0, 0.0).astype(BF16)
        turned = lax.dot_general(
            pick, flat, (((1,), (1,)), ((), ())), preferred_element_type=F32
        )
        halves = [turned[:, :128], turned[:, 128:]]
        rolled.append(
            [[h if s == 0 else pltpu.roll(h, 32 * s, 1) for s in range(4)] for h in halves]
        )
    lane_group = lax.broadcasted_iota(jnp.int32, (BLOCKS, 128), 1) // 32
    for f in range(LOCAL):
        for part in range(2):
            value = None
            for g in range(4):
                piece = rolled[part * 4 + g][f // 4][(g - f % 4) % 4]
                value = piece if value is None else jnp.where(lane_group == g, piece, value)
            (low_ref, high_ref)[part][pl.ds(f, BLOCKS, stride=LOCAL), :] = value
    count = TILES * LOCAL
    for at, source, start in (
        (0, low_ref, 0),
        (128, high_ref, 0),
        (256, low_ref, 8),
        (384, high_ref, 8),
        (512, low_ref, 16),
    ):
        out_ref[:, at : at + 128] = source[start : start + count, :].astype(BF16)


def pack(frames, mask):
    return pl.pallas_call(
        pack_kernel,
        out_shape=jax.ShapeDtypeStruct((TILES * LOCAL, WIDE * ROWS), BF16),
        scratch_shapes=[pltpu.VMEM((BLOCKS * LOCAL, 128), F32)] * 2,
        compiler_params=pltpu.CompilerParams(vmem_limit_bytes=32 * 1024 * 1024),
    )(frames, mask)


def spectra_kernel(series_ref, table_ref, own_ref, last_ref, first_ref):
    spectrum = lax.dot_general(
        series_ref[...],
        table_ref[...],
        (((0,), (0,)), ((), ())),
        preferred_element_type=F32,
    )
    own_ref[...] = spectrum.astype(BF16)
    by_column = spectrum.reshape(WIDE, ROWS, 2 * FREQ)
    last_ref[...] = by_column[:, ROWS - 8 :].reshape(WIDE * 8, 2 * FREQ).astype(BF16)
    first_ref[...] = by_column[:, :8].reshape(WIDE * 8, 2 * FREQ).astype(BF16)


def spectra(series, table):
    edge = jax.ShapeDtypeStruct((WIDE * 8, 2 * FREQ), BF16)
    return pl.pallas_call(
        spectra_kernel,
        out_shape=(jax.ShapeDtypeStruct((WIDE * ROWS, 2 * FREQ), BF16), edge, edge),
        compiler_params=pltpu.CompilerParams(vmem_limit_bytes=32 * 1024 * 1024),
    )(series, table)


def cross_kernel(
    offsets_ref,
    own_ref,
    before_ref,
    after_ref,
    mask_ref,
    gain_ref,
    mix_ref,
    out_ref,
    tall_re,
    tall_im,
    filt_re,
    filt_im,
    centre_re,
    centre_im,
    sums,
    seen,
):
    own = own_ref[...].astype(F32).reshape(WIDE, ROWS, 2 * FREQ)
    before = before_ref[...].astype(F32).reshape(WIDE, 8, 2 * FREQ)
    after = after_ref[...].astype(F32).reshape(WIDE, 8, 2 * FREQ)
    for q in range(WIDE):
        for tall, low in ((tall_re, 0), (tall_im, FREQ)):
            lanes = slice(low, low + FREQ)
            tall[q * TALL : q * TALL + 8, :] = before[q, :, lanes]
            tall[q * TALL + 8 : q * TALL + 40, :] = own[q, :, lanes]
            tall[q * TALL + 40 : q * TALL + 48, :] = after[q, :, lanes]

    gain = gain_ref[...]
    mix = mix_ref[...]
    for tall, filt in ((tall_re, filt_re), (tall_im, filt_im)):
        for q in range(SIDE):
            at = (q + 2) * TALL + 4
            inner = tall[at : at + REACH, :]
            beside = 0.25 * (
                tall[at + 1 : at + 1 + REACH, :]
                + tall[at - 1 : at - 1 + REACH, :]
                + tall[at + TALL : at + TALL + REACH, :]
                + tall[at - TALL : at - TALL + REACH, :]
            )
            filt[q * REACH : (q + 1) * REACH, :] = gain * inner + mix * (beside - inner)

    tile = lax.axis_index("tile")
    wide = pl.multiple_of((tile // 16) * 128, 128)
    near = mask_ref[:, pl.ds(wide, 128)].astype(F32)
    near = pltpu.roll(near, (128 - 8 * (tile % 16)) % 128, 1)
    for part in range(2):
        total = jnp.zeros((ROWS, 128), F32)
        for c in range(part * 4, part * 4 + 4):
            weight = jnp.broadcast_to(near[:, c : c + 1], (ROWS, 128))
            total = total + weight
            at = (c + 4) * REACH + 4
            centre_re[c * ROWS : (c + 1) * ROWS, :] = filt_re[at : at + ROWS, :] * weight
            centre_im[c * ROWS : (c + 1) * ROWS, :] = filt_im[at : at + ROWS, :] * weight
        seen[part * ROWS : (part + 1) * ROWS, :] = total

    def distance(d, carry):
        starts = [offsets_ref[d * OFFS + k] for k in range(OFFS)]
        for part in range(2):
            first = jnp.zeros((ROWS, 128), F32)
            second = jnp.zeros((ROWS, 128), F32)
            for c in range(part * 4, part * 4 + 4):
                real_a = filt_re[pl.ds(starts[0] + c * REACH, ROWS), :]
                imag_a = filt_im[pl.ds(starts[0] + c * REACH, ROWS), :]
                for k in range(1, OFFS):
                    real_a = real_a + filt_re[pl.ds(starts[k] + c * REACH, ROWS), :]
                    imag_a = imag_a + filt_im[pl.ds(starts[k] + c * REACH, ROWS), :]
                real_c = centre_re[c * ROWS : (c + 1) * ROWS, :]
                imag_c = centre_im[c * ROWS : (c + 1) * ROWS, :]
                first = first + (real_c * real_a + imag_c * imag_a)
                second = second + (real_c * imag_a - imag_c * real_a)
            for group in range(4):
                at = pl.multiple_of(((group * 2 + part) * 16 + 2 * d) * 8, 8)
                sums[pl.ds(at, 8), :] = first[group * 8 : group * 8 + 8]
                sums[pl.ds(at + 8, 8), :] = second[group * 8 : group * 8 + 8]
        return carry

    lax.fori_loop(0, DIST, distance, 0)

    for group in range(4):
        for half in range(2):
            for part in range(2):
                at = part * ROWS + group * 8 + half * 4
                count = seen[at : at + 1, :]
                for k in range(1, 4):
                    count = count + seen[at + k : at + k + 1, :]
                denom = jnp.broadcast_to(jnp.maximum(count, 1.0), (8, 128))
                for piece in range(2):
                    base = ((group * 2 + part) * 16 + piece * 8) * 8 + half * 4
                    total = sums[pl.ds(base, 8, stride=8), :]
                    for k in range(1, 4):
                        total = total + sums[pl.ds(base + k, 8, stride=8), :]
                    row = ((group * 2 + half) * 2 + part) * 16 + piece * 8
                    out_ref[row : row + 8, :] = total / denom


def cross_spectra(starts, own, before, after, mask, gain, mix):
    vmem = pl.BlockSpec(memory_space=pltpu.VMEM)
    return pl.pallas_call(
        cross_kernel,
        out_shape=jax.ShapeDtypeStruct((8 * 2 * DIST * 2, FREQ), F32),
        in_specs=[pl.BlockSpec(memory_space=pltpu.SMEM)] + [vmem] * 6,
        scratch_shapes=[
            pltpu.VMEM((WIDE * TALL, FREQ), F32),
            pltpu.VMEM((WIDE * TALL, FREQ), F32),
            pltpu.VMEM((SIDE * REACH, FREQ), F32),
            pltpu.VMEM((SIDE * REACH, FREQ), F32),
            pltpu.VMEM((COLS * ROWS, FREQ), F32),
            pltpu.VMEM((COLS * ROWS, FREQ), F32),
            pltpu.VMEM((8 * 16 * 8, FREQ), F32),
            pltpu.VMEM((2 * ROWS, FREQ), F32),
        ],
        compiler_params=pltpu.CompilerParams(vmem_limit_bytes=32 * 1024 * 1024),
    )(starts, own, before, after, mask, gain, mix)


def on_device(frames, disk_mask, offsets, filter_gain, filter_mix):
    packed = pack(frames, disk_mask).reshape(TILES, LOCAL, WIDE * ROWS)
    received = lax.all_to_all(packed, "tile", split_axis=0, concat_axis=0, tiled=True)
    series = received.reshape(FRAMES, WIDE * ROWS)
    own, last, first = spectra(series, dft_table())
    bands = lax.axis_size("band")
    up = [(i, i + 1) for i in range(bands - 1)]
    down = [(j, i) for i, j in up]
    before = lax.ppermute(last, "band", up)
    after = lax.ppermute(first, "band", down)
    starts = ((offsets[..., 1] + 4) * REACH + offsets[..., 0] + 4).reshape(DIST * OFFS)
    out = cross_spectra(
        starts,
        own,
        before,
        after,
        disk_mask,
        filter_gain.reshape(1, FREQ),
        filter_mix.reshape(1, FREQ),
    )
    return out.reshape(8, 2, DIST, 2, FREQ)


def solution(mesh):
    return jax.shard_map(
        on_device,
        mesh=mesh,
        in_specs=(P("tile", "band", None), P("band", None), P(), P(), P()),
        out_specs=P("band", "tile", None, None, None),
        check_vma=False,
    )
```

```python
import math

import jax
import jax.numpy as jnp
import numpy as np
from jax import lax
from jax.experimental import pallas as pl
from jax.experimental.pallas import tpu as pltpu
from jax.sharding import PartitionSpec as P

FRAMES = 512
FREQ = 128
DIST = 8
OFFS = 8
FLO = 48
TILES = 64
LOCAL = 8
ROWS = 32
COLS = 8
WIDE = 20
LEAD = 6
BLOCKS = 72
TALL = 48
REACH = 40
SIDE = 16

F32 = jnp.float32
BF16 = jnp.bfloat16


def dft_table():
    times = np.arange(FRAMES, dtype=np.int32)
    freqs = FLO + np.arange(FREQ, dtype=np.int32)
    phases = times[:, None] * freqs[None, :] % FRAMES
    angles = phases.astype(np.float32) * np.float32(2.0 * math.pi / FRAMES)
    factor = np.float32(1.0 / math.sqrt(FRAMES))
    both = np.concatenate([np.cos(angles) * factor, -np.sin(angles) * factor], axis=1)
    return jnp.asarray(both.astype(np.float32)).astype(BF16)


def pack_kernel(frames_ref, mask_ref, out_ref, frames_vmem, mask_vmem, pick_ref, low_ref, high_ref, sems):
    copies = [
        pltpu.make_async_copy(mask_ref, mask_vmem, sems.at[0]),
        pltpu.make_async_copy(frames_ref, frames_vmem, sems.at[1]),
    ]
    for copy in copies:
        copy.start()
    width = mask_vmem.shape[1]
    cols = lax.broadcasted_iota(jnp.int32, (BLOCKS, width), 1)
    block = lax.broadcasted_iota(jnp.int32, (BLOCKS, width), 0)
    place = cols - 8 * block + LEAD
    for c in range(COLS):
        pick_ref[c] = jnp.where(place == c, 1.0, 0.0)
    for copy in copies:
        copy.wait()
    mask = mask_vmem[...].astype(F32)
    masked = (frames_vmem[...].astype(F32) * mask[None]).astype(BF16)
    flat = masked.reshape(LOCAL * ROWS, width)
    rolled = []
    for c in range(COLS):
        turned = lax.dot_general(
            pick_ref[c].astype(BF16), flat, (((1,), (1,)), ((), ())), preferred_element_type=F32
        )
        halves = [turned[:, :128], turned[:, 128:]]
        rolled.append(
            [[h if s == 0 else pltpu.roll(h, 32 * s, 1) for s in range(4)] for h in halves]
        )
    lane_group = lax.broadcasted_iota(jnp.int32, (BLOCKS, 128), 1) // 32
    for f in range(LOCAL):
        for part in range(2):
            value = None
            for g in range(4):
                piece = rolled[part * 4 + g][f // 4][(g - f % 4) % 4]
                value = piece if value is None else jnp.where(lane_group == g, piece, value)
            (low_ref, high_ref)[part][pl.ds(f, BLOCKS, stride=LOCAL), :] = value
    count = TILES * LOCAL
    for at, source, start in (
        (0, low_ref, 0),
        (128, high_ref, 0),
        (256, low_ref, 8),
        (384, high_ref, 8),
        (512, low_ref, 16),
    ):
        out_ref[:, at : at + 128] = source[start : start + count, :].astype(BF16)


def pack(frames, mask):
    return pl.pallas_call(
        pack_kernel,
        out_shape=pltpu.VMEM((TILES * LOCAL, WIDE * ROWS), BF16),
        in_specs=[pl.BlockSpec(memory_space=pltpu.HBM)] * 2,
        scratch_shapes=[
            pltpu.VMEM(frames.shape, BF16),
            pltpu.VMEM(mask.shape, jnp.int32),
            pltpu.VMEM((COLS, BLOCKS, mask.shape[1]), F32),
            pltpu.VMEM((BLOCKS * LOCAL, 128), F32),
            pltpu.VMEM((BLOCKS * LOCAL, 128), F32),
            pltpu.SemaphoreType.DMA((2,)),
        ],
        compiler_params=pltpu.CompilerParams(vmem_limit_bytes=60000000),
    )(frames, mask)


def spectra_kernel(series_ref, table_ref, own_ref, last_ref, first_ref):
    spectrum = lax.dot_general(
        series_ref[...],
        table_ref[...],
        (((0,), (0,)), ((), ())),
        preferred_element_type=F32,
    )
    own_ref[...] = spectrum.astype(BF16)
    by_column = spectrum.reshape(WIDE, ROWS, 2 * FREQ)
    last_ref[...] = by_column[:, ROWS - 8 :].reshape(WIDE * 8, 2 * FREQ).astype(BF16)
    first_ref[...] = by_column[:, :8].reshape(WIDE * 8, 2 * FREQ).astype(BF16)


def spectra(series, table):
    edge = jax.ShapeDtypeStruct((WIDE * 8, 2 * FREQ), BF16)
    return pl.pallas_call(
        spectra_kernel,
        out_shape=(jax.ShapeDtypeStruct((WIDE * ROWS, 2 * FREQ), BF16), edge, edge),
        compiler_params=pltpu.CompilerParams(vmem_limit_bytes=32 * 1024 * 1024),
    )(series, table)


def filtered(tall, at, rows, gain, mix):
    rim = tall[1]
    tall = tall[0]
    inner = tall[at : at + rows, :]
    beside = 0.25 * (
        tall[at + 1 : at + 1 + rows, :]
        + tall[at - 1 : at - 1 + rows, :]
        + tall[at + rim : at + rim + rows, :]
        + tall[at - rim : at - rim + rows, :]
    )
    return gain * inner + mix * (beside - inner)


def block_rows(groups, offsets_ref, filt_re, filt_im, centre_re, centre_im, sums):
    at_group = {group: n for n, group in enumerate(groups)}

    def distance(d, carry):
        starts = [offsets_ref[d * OFFS + k] for k in range(OFFS)]
        for part in range(2):
            for group in groups:
                first = jnp.zeros((8, 128), F32)
                second = jnp.zeros((8, 128), F32)
                for c in range(part * 4, part * 4 + 4):
                    shift = c * REACH + group * 8
                    real_a = filt_re[pl.ds(starts[0] + shift, 8), :]
                    imag_a = filt_im[pl.ds(starts[0] + shift, 8), :]
                    for k in range(1, OFFS):
                        real_a = real_a + filt_re[pl.ds(starts[k] + shift, 8), :]
                        imag_a = imag_a + filt_im[pl.ds(starts[k] + shift, 8), :]
                    at = c * ROWS + group * 8
                    real_c = centre_re[at : at + 8, :]
                    imag_c = centre_im[at : at + 8, :]
                    first = first + (real_c * real_a + imag_c * imag_a)
                    second = second + (real_c * imag_a - imag_c * real_a)
                at = pl.multiple_of(((at_group[group] * 2 + part) * 16 + 2 * d) * 8, 8)
                sums[pl.ds(at, 8), :] = first
                sums[pl.ds(at + 8, 8), :] = second
        return carry

    lax.fori_loop(0, DIST, distance, 0)


def block_means(groups, sums, seen, out_ref, first_row):
    for n, group in enumerate(groups):
        for half in range(2):
            for part in range(2):
                at = part * ROWS + group * 8 + half * 4
                count = seen[at : at + 1, :]
                for k in range(1, 4):
                    count = count + seen[at + k : at + k + 1, :]
                denom = jnp.broadcast_to(jnp.maximum(count, 1.0), (8, 128))
                for piece in range(2):
                    base = ((n * 2 + part) * 16 + piece * 8) * 8 + half * 4
                    total = sums[pl.ds(base, 8, stride=8), :]
                    for k in range(1, 4):
                        total = total + sums[pl.ds(base + k, 8, stride=8), :]
                    row = ((group * 2 + half) * 2 + part) * 16 + piece * 8 - first_row
                    out_ref[row : row + 8, :] = total / denom


def middle_kernel(
    offsets_ref,
    own_ref,
    mask_ref,
    gain_ref,
    mix_ref,
    out_ref,
    filt_re,
    filt_im,
    seen,
    pair_ref,
    own_re,
    own_im,
    centre_re,
    centre_im,
    sums,
):
    own_re[...] = own_ref[:, :FREQ].astype(F32)
    own_im[...] = own_ref[:, FREQ:].astype(F32)
    gain = gain_ref[...]
    mix = mix_ref[...]
    pair_ref[0:1, :] = gain
    pair_ref[1:2, :] = mix
    for source, filt in ((own_re, filt_re), (own_im, filt_im)):
        for q in range(SIDE):
            at = (q + 2) * ROWS + 1
            value = filtered((source, ROWS), at, ROWS - 2, gain, mix)
            filt[q * REACH + 5 : q * REACH + 5 + ROWS - 2, :] = value

    tile = lax.axis_index("tile")
    wide = pl.multiple_of((tile // 16) * 128, 128)
    near = mask_ref[:, pl.ds(wide, 128)].astype(F32)
    near = pltpu.roll(near, (128 - 8 * (tile % 16)) % 128, 1)
    for part in range(2):
        total = jnp.zeros((ROWS, 128), F32)
        for c in range(part * 4, part * 4 + 4):
            weight = jnp.broadcast_to(near[:, c : c + 1], (ROWS, 128))
            total = total + weight
            at = (c + 4) * REACH + 12
            to = c * ROWS + 8
            centre_re[to : to + 16, :] = filt_re[at : at + 16, :] * weight[8:24]
            centre_im[to : to + 16, :] = filt_im[at : at + 16, :] * weight[8:24]
            pair_ref[8 + c * 8 : 16 + c * 8, :] = weight[0:8]
            pair_ref[72 + c * 8 : 80 + c * 8, :] = weight[24:32]
        seen[part * ROWS : (part + 1) * ROWS, :] = total

    groups = (1, 2)
    block_rows(groups, offsets_ref, filt_re, filt_im, centre_re, centre_im, sums)
    block_means(groups, sums, seen, out_ref, 64)


def outer_kernel(
    offsets_ref,
    before_ref,
    first_ref,
    last_ref,
    after_ref,
    mid_ref,
    own_filt_re,
    own_filt_im,
    seen,
    pair_ref,
    out_ref,
    top_re,
    top_im,
    low_re,
    low_im,
    filt_re,
    filt_im,
    centre_re,
    centre_im,
    sums,
):
    for upper, lower, real, imag in (
        (before_ref, first_ref, top_re, top_im),
        (last_ref, after_ref, low_re, low_im),
    ):
        for at, ref in ((0, upper), (8, lower)):
            value = ref[...].astype(F32).reshape(WIDE, 8, 2 * FREQ)
            for q in range(WIDE):
                real[q * 16 + at : q * 16 + at + 8, :] = value[q, :, :FREQ]
                imag[q * 16 + at : q * 16 + at + 8, :] = value[q, :, FREQ:]
    gain = pair_ref[0:1, :]
    mix = pair_ref[1:2, :]
    for top, low, inside, filt in (
        (top_re, low_re, own_filt_re, filt_re),
        (top_im, low_im, own_filt_im, filt_im),
    ):
        for q in range(SIDE):
            at = q * REACH
            filt[at : at + 8, :] = filtered((top, 16), (q + 2) * 16 + 4, 8, gain, mix)
            filt[at + 8 : at + 32, :] = inside[at + 8 : at + 32, :]
            filt[at + 32 : at + 40, :] = filtered((low, 16), (q + 2) * 16 + 4, 8, gain, mix)
    for c in range(COLS):
        at = (c + 4) * REACH + 4
        for weight_at, row in ((8, 0), (72, 24)):
            weight = pair_ref[weight_at + c * 8 : weight_at + c * 8 + 8, :]
            to = c * ROWS + row
            centre_re[to : to + 8, :] = filt_re[at + row : at + row + 8, :] * weight
            centre_im[to : to + 8, :] = filt_im[at + row : at + row + 8, :] * weight

    groups = (0, 3)
    block_rows(groups, offsets_ref, filt_re, filt_im, centre_re, centre_im, sums)
    out_ref[64:192, :] = mid_ref[...]
    block_means(groups, sums, seen, out_ref, 0)


def float_shape(rows):
    return jax.ShapeDtypeStruct((rows, FREQ), F32)


def middle(starts, own, mask, gain, mix):
    vmem = pl.BlockSpec(memory_space=pltpu.VMEM)
    rows = (128, SIDE * REACH, SIDE * REACH, 2 * ROWS, 136)
    return pl.pallas_call(
        middle_kernel,
        out_shape=tuple(float_shape(n) for n in rows),
        in_specs=[pl.BlockSpec(memory_space=pltpu.SMEM)] + [vmem] * 4,
        scratch_shapes=[
            pltpu.VMEM((WIDE * ROWS, FREQ), F32),
            pltpu.VMEM((WIDE * ROWS, FREQ), F32),
            pltpu.VMEM((COLS * ROWS, FREQ), F32),
            pltpu.VMEM((COLS * ROWS, FREQ), F32),
            pltpu.VMEM((4 * 16 * 8, FREQ), F32),
        ],
        compiler_params=pltpu.CompilerParams(vmem_limit_bytes=32 * 1024 * 1024),
        cost_estimate=pl.CostEstimate(flops=6_000_000, bytes_accessed=4_000_000, transcendentals=0),
    )(starts, own, mask, gain, mix)


def outer(starts, before, first, last, after, kept):
    vmem = pl.BlockSpec(memory_space=pltpu.VMEM)
    rows = [WIDE * 16] * 4 + [SIDE * REACH] * 2 + [COLS * ROWS] * 2 + [4 * 16 * 8]
    return pl.pallas_call(
        outer_kernel,
        out_shape=float_shape(8 * 2 * DIST * 2),
        in_specs=[pl.BlockSpec(memory_space=pltpu.SMEM)] + [vmem] * (4 + len(kept)),
        scratch_shapes=[pltpu.VMEM((n, FREQ), F32) for n in rows],
        compiler_params=pltpu.CompilerParams(vmem_limit_bytes=32 * 1024 * 1024),
    )(starts, before, first, last, after, *kept)


def on_device(frames, disk_mask, offsets, filter_gain, filter_mix):
    packed = pack(frames, disk_mask).reshape(TILES, LOCAL, WIDE * ROWS)
    received = lax.all_to_all(packed, "tile", split_axis=0, concat_axis=0, tiled=True)
    series = received.reshape(FRAMES, WIDE * ROWS)
    own, last, first = spectra(series, dft_table())
    bands = lax.axis_size("band")
    up = [(i, i + 1) for i in range(bands - 1)]
    down = [(j, i) for i, j in up]
    before = lax.ppermute(last, "band", up)
    after = lax.ppermute(first, "band", down)
    starts = ((offsets[..., 1] + 4) * REACH + offsets[..., 0] + 4).reshape(DIST * OFFS)
    gain = filter_gain.reshape(1, FREQ)
    mix = filter_mix.reshape(1, FREQ)
    kept = middle(starts, own, disk_mask, gain, mix)
    out = outer(starts, before, first, last, after, kept)
    return out.reshape(8, 2, DIST, 2, FREQ)


def solution(mesh):
    return jax.shard_map(
        on_device,
        mesh=mesh,
        in_specs=(P("tile", "band", None), P("band", None), P(), P(), P()),
        out_specs=P("band", "tile", None, None, None),
        check_vma=False,
    )
```

```python
import math

import jax
import jax.numpy as jnp
import numpy as np
from jax import lax
from jax.experimental import pallas as pl
from jax.experimental.pallas import tpu as pltpu
from jax.sharding import PartitionSpec as P

FRAMES = 512
FREQ = 128
DIST = 8
OFFS = 8
FLO = 48
TILES = 64
LOCAL = 8
ROWS = 32
COLS = 8
WIDE = 20
LEAD = 6
BLOCKS = 72
TALL = 48
REACH = 40
SIDE = 16

F32 = jnp.float32
BF16 = jnp.bfloat16


def dft_table():
    times = np.arange(FRAMES, dtype=np.int32)
    freqs = FLO + np.arange(FREQ, dtype=np.int32)
    phases = times[:, None] * freqs[None, :] % FRAMES
    angles = phases.astype(np.float32) * np.float32(2.0 * math.pi / FRAMES)
    factor = np.float32(1.0 / math.sqrt(FRAMES))
    both = np.concatenate([np.cos(angles) * factor, -np.sin(angles) * factor], axis=1)
    return jnp.asarray(both.astype(np.float32)).astype(BF16)


def pack_kernel(frames_ref, mask_ref, out_ref, frames_vmem, mask_vmem, pick_ref, low_ref, high_ref, sems):
    near = LOCAL // 2
    copies = [
        pltpu.make_async_copy(mask_ref, mask_vmem, sems.at[0]),
        pltpu.make_async_copy(frames_ref.at[:near], frames_vmem.at[:near], sems.at[1]),
        pltpu.make_async_copy(frames_ref.at[near:], frames_vmem.at[near:], sems.at[2]),
    ]
    for copy in copies:
        copy.start()
    width = mask_vmem.shape[1]
    cols = lax.broadcasted_iota(jnp.int32, (BLOCKS, width), 1)
    block = lax.broadcasted_iota(jnp.int32, (BLOCKS, width), 0)
    place = cols - 8 * block + LEAD
    for c in range(COLS):
        pick_ref[c] = jnp.where(place == c, 1.0, 0.0)
    copies[0].wait()
    mask = mask_vmem[...].astype(F32)
    lane_group = lax.broadcasted_iota(jnp.int32, (BLOCKS, 128), 1) // 32
    for half in range(2):
        copies[1 + half].wait()
        chosen = frames_vmem[half * near : (half + 1) * near].astype(F32)
        flat = (chosen * mask[None]).astype(BF16).reshape(near * ROWS, width)
        rolled = []
        for c in range(COLS):
            turned = lax.dot_general(
                pick_ref[c].astype(BF16),
                flat,
                (((1,), (1,)), ((), ())),
                preferred_element_type=F32,
            )
            rolled.append([turned if n == 0 else pltpu.roll(turned, 32 * n, 1) for n in range(4)])
        for f in range(near):
            for part in range(2):
                value = None
                for g in range(4):
                    piece = rolled[part * 4 + g][(g - f) % 4]
                    value = piece if value is None else jnp.where(lane_group == g, piece, value)
                at = half * near + f
                (low_ref, high_ref)[part][pl.ds(at, BLOCKS, stride=LOCAL), :] = value
    count = TILES * LOCAL
    for at, source, start in (
        (0, low_ref, 0),
        (128, high_ref, 0),
        (256, low_ref, 8),
        (384, high_ref, 8),
        (512, low_ref, 16),
    ):
        out_ref[:, at : at + 128] = source[start : start + count, :].astype(BF16)


def pack(frames, mask):
    return pl.pallas_call(
        pack_kernel,
        out_shape=pltpu.VMEM((TILES * LOCAL, WIDE * ROWS), BF16),
        in_specs=[pl.BlockSpec(memory_space=pltpu.HBM)] * 2,
        scratch_shapes=[
            pltpu.VMEM(frames.shape, BF16),
            pltpu.VMEM(mask.shape, jnp.int32),
            pltpu.VMEM((COLS, BLOCKS, mask.shape[1]), F32),
            pltpu.VMEM((BLOCKS * LOCAL, 128), F32),
            pltpu.VMEM((BLOCKS * LOCAL, 128), F32),
            pltpu.SemaphoreType.DMA((3,)),
        ],
        compiler_params=pltpu.CompilerParams(vmem_limit_bytes=60000000),
    )(frames, mask)


def spectra_kernel(series_ref, table_ref, own_ref, even_ref, odd_ref):
    spectrum = lax.dot_general(
        series_ref[...],
        table_ref[...],
        (((0,), (0,)), ((), ())),
        preferred_element_type=F32,
    )
    own_ref[...] = spectrum.astype(BF16)
    by_column = spectrum.reshape(WIDE, ROWS, 2 * FREQ)
    last = by_column[:, ROWS - 8 :].reshape(WIDE * 8, 2 * FREQ).astype(BF16)
    first = by_column[:, :8].reshape(WIDE * 8, 2 * FREQ).astype(BF16)
    odd_band = lax.axis_index("band") % 2

    @pl.when(odd_band == 0)
    def _():
        even_ref[...] = last
        odd_ref[...] = first

    @pl.when(odd_band == 1)
    def _():
        even_ref[...] = first
        odd_ref[...] = last


def spectra(series, table):
    edge = jax.ShapeDtypeStruct((WIDE * 8, 2 * FREQ), BF16)
    return pl.pallas_call(
        spectra_kernel,
        out_shape=(jax.ShapeDtypeStruct((WIDE * ROWS, 2 * FREQ), BF16), edge, edge),
        compiler_params=pltpu.CompilerParams(vmem_limit_bytes=32 * 1024 * 1024),
    )(series, table)


def filtered(tall, at, rows, gain, mix):
    rim = tall[1]
    tall = tall[0]
    inner = tall[at : at + rows, :]
    beside = 0.25 * (
        tall[at + 1 : at + 1 + rows, :]
        + tall[at - 1 : at - 1 + rows, :]
        + tall[at + rim : at + rim + rows, :]
        + tall[at - rim : at - rim + rows, :]
    )
    return gain * inner + mix * (beside - inner)


def block_rows(rows, offsets_ref, filt_re, filt_im, centre_re, centre_im, sums):
    def distance(d, carry):
        starts = [offsets_ref[d * OFFS + k] for k in range(OFFS)]
        for n, row in enumerate(rows):
            for part in range(2):
                first = jnp.zeros((8, 128), F32)
                second = jnp.zeros((8, 128), F32)
                for c in range(part * 4, part * 4 + 4):
                    shift = c * REACH + row
                    real_a = filt_re[pl.ds(starts[0] + shift, 8), :]
                    imag_a = filt_im[pl.ds(starts[0] + shift, 8), :]
                    for k in range(1, OFFS):
                        real_a = real_a + filt_re[pl.ds(starts[k] + shift, 8), :]
                        imag_a = imag_a + filt_im[pl.ds(starts[k] + shift, 8), :]
                    at = (n * COLS + c) * 8
                    real_c = centre_re[at : at + 8, :]
                    imag_c = centre_im[at : at + 8, :]
                    first = first + (real_c * real_a + imag_c * imag_a)
                    second = second + (real_c * imag_a - imag_c * real_a)
                at = pl.multiple_of(((n * 2 + part) * 16 + 2 * d) * 8, 8)
                sums[pl.ds(at, 8), :] = first
                sums[pl.ds(at + 8, 8), :] = second
        return carry

    lax.fori_loop(0, DIST, distance, 0)


def block_means(rows, sums, seen, out_ref):
    for n, row in enumerate(rows):
        for half in range(2):
            for part in range(2):
                at = row + part * ROWS + half * 4
                count = seen[pl.ds(at, 1), :]
                for k in range(1, 4):
                    count = count + seen[pl.ds(at + k, 1), :]
                denom = jnp.broadcast_to(jnp.maximum(count, 1.0), (8, 128))
                for piece in range(2):
                    base = ((n * 2 + part) * 16 + piece * 8) * 8 + half * 4
                    total = sums[pl.ds(base, 8, stride=8), :]
                    for k in range(1, 4):
                        total = total + sums[pl.ds(base + k, 8, stride=8), :]
                    to = ((n * 2 + half) * 2 + part) * 16 + piece * 8
                    out_ref[to : to + 8, :] = total / denom


def middle_kernel(
    offsets_ref,
    own_ref,
    mask_ref,
    gain_ref,
    mix_ref,
    out_ref,
    filt_re,
    filt_im,
    seen,
    pair_ref,
    own_re,
    own_im,
    centre_re,
    centre_im,
    sums,
):
    own_re[...] = own_ref[:, :FREQ].astype(F32)
    own_im[...] = own_ref[:, FREQ:].astype(F32)
    gain = gain_ref[...]
    mix = mix_ref[...]
    pair_ref[0:1, :] = gain
    pair_ref[1:2, :] = mix
    for source, filt in ((own_re, filt_re), (own_im, filt_im)):
        for q in range(SIDE):
            at = (q + 2) * ROWS + 1
            value = filtered((source, ROWS), at, ROWS - 2, gain, mix)
            filt[q * REACH + 5 : q * REACH + 5 + ROWS - 2, :] = value

    tile = lax.axis_index("tile")
    wide = pl.multiple_of((tile // 16) * 128, 128)
    near = mask_ref[:, pl.ds(wide, 128)].astype(F32)
    near = pltpu.roll(near, (128 - 8 * (tile % 16)) % 128, 1)
    for part in range(2):
        total = jnp.zeros((ROWS, 128), F32)
        for c in range(part * 4, part * 4 + 4):
            weight = jnp.broadcast_to(near[:, c : c + 1], (ROWS, 128))
            total = total + weight
            for n, row in enumerate((8, 16)):
                at = (c + 4) * REACH + 4 + row
                to = (n * COLS + c) * 8
                centre_re[to : to + 8, :] = filt_re[at : at + 8, :] * weight[row : row + 8]
                centre_im[to : to + 8, :] = filt_im[at : at + 8, :] * weight[row : row + 8]
            pair_ref[8 + c * 8 : 16 + c * 8, :] = weight[0:8]
            pair_ref[72 + c * 8 : 80 + c * 8, :] = weight[24:32]
        seen[part * ROWS : (part + 1) * ROWS, :] = total

    rows = (8, 16)
    block_rows(rows, offsets_ref, filt_re, filt_im, centre_re, centre_im, sums)
    block_means(rows, sums, seen, out_ref)


def edge_rows(
    top,
    offsets_ref,
    came_ref,
    went_ref,
    own_filt_re,
    own_filt_im,
    seen,
    pair_ref,
    result,
    tall_re,
    tall_im,
    filt_re,
    filt_im,
    centre_re,
    centre_im,
    sums,
):
    for at, ref in ((8 - 8 * top, came_ref), (8 * top, went_ref)):
        value = ref[...].astype(F32).reshape(WIDE, 8, 2 * FREQ)
        at = pl.multiple_of(at, 8)
        for q in range(WIDE):
            tall_re[pl.ds(at + q * 16, 8), :] = value[q, :, :FREQ]
            tall_im[pl.ds(at + q * 16, 8), :] = value[q, :, FREQ:]
    gain = pair_ref[0:1, :]
    mix = pair_ref[1:2, :]
    edge = pl.multiple_of(32 - 32 * top, 8)
    kept = pl.multiple_of(24 - 16 * top, 8)
    row = pl.multiple_of(24 - 24 * top, 8)
    for tall, inside, filt in ((tall_re, own_filt_re, filt_re), (tall_im, own_filt_im, filt_im)):
        for q in range(SIDE):
            at = q * REACH
            filt[pl.ds(edge + at, 8), :] = filtered((tall, 16), (q + 2) * 16 + 4, 8, gain, mix)
            filt[pl.ds(kept + at, 8), :] = inside[pl.ds(kept + at, 8), :]
    for c in range(COLS):
        weight = pair_ref[pl.ds(pl.multiple_of(72 - 64 * top, 8) + c * 8, 8), :]
        at = (c + 4) * REACH + 4
        centre_re[c * 8 : c * 8 + 8, :] = filt_re[pl.ds(row + at, 8), :] * weight
        centre_im[c * 8 : c * 8 + 8, :] = filt_im[pl.ds(row + at, 8), :] * weight
    block_rows((row,), offsets_ref, filt_re, filt_im, centre_re, centre_im, sums)
    block_means((row,), sums, seen, result)


def edge_kernel(*refs):
    edge_rows(lax.axis_index("band") % 2, *refs)


def last_kernel(offsets_ref, came_ref, went_ref, filt_re, filt_im, seen, pair_ref, mid_ref, edge_ref, out_ref, result, *rest):
    sems = rest[-1]
    top = 1 - lax.axis_index("band") % 2
    there = pl.multiple_of(192 * top, 64)
    here = pl.multiple_of(192 - 192 * top, 64)
    copies = [
        pltpu.make_async_copy(mid_ref, out_ref.at[pl.ds(64, 128)], sems.at[0]),
        pltpu.make_async_copy(edge_ref, out_ref.at[pl.ds(there, 64)], sems.at[1]),
        pltpu.make_async_copy(result, out_ref.at[pl.ds(here, 64)], sems.at[2]),
    ]
    copies[0].start()
    copies[1].start()
    edge_rows(
        top, offsets_ref, came_ref, went_ref, filt_re, filt_im, seen, pair_ref, result, *rest[:-1]
    )
    copies[2].start()
    for copy in copies:
        copy.wait()


def float_shape(rows):
    return jax.ShapeDtypeStruct((rows, FREQ), F32)


def middle(starts, own, mask, gain, mix):
    vmem = pl.BlockSpec(memory_space=pltpu.VMEM)
    rows = (128, SIDE * REACH, SIDE * REACH, 2 * ROWS, 136)
    return pl.pallas_call(
        middle_kernel,
        out_shape=tuple(float_shape(n) for n in rows),
        in_specs=[pl.BlockSpec(memory_space=pltpu.SMEM)] + [vmem] * 4,
        scratch_shapes=[
            pltpu.VMEM((WIDE * ROWS, FREQ), F32),
            pltpu.VMEM((WIDE * ROWS, FREQ), F32),
            pltpu.VMEM((2 * COLS * 8, FREQ), F32),
            pltpu.VMEM((2 * COLS * 8, FREQ), F32),
            pltpu.VMEM((4 * 16 * 8, FREQ), F32),
        ],
        compiler_params=pltpu.CompilerParams(vmem_limit_bytes=32 * 1024 * 1024),
        cost_estimate=pl.CostEstimate(flops=6_000_000, bytes_accessed=4_000_000, transcendentals=0),
    )(starts, own, mask, gain, mix)


def edges(starts, even, odd, kept):
    vmem = pl.BlockSpec(memory_space=pltpu.VMEM)
    smem = pl.BlockSpec(memory_space=pltpu.SMEM)
    bands = lax.axis_size("band")
    pairs = [(i, i ^ 1) for i in range(bands)]
    between = [(i, ((i + 1) ^ 1) - 1) for i in range(1, bands - 1)]
    came_even = lax.ppermute(even, "band", pairs)
    came_odd = lax.ppermute(odd, "band", between)
    mid, *shared = kept
    rows = [WIDE * 16] * 2 + [SIDE * REACH] * 2 + [COLS * 8] * 2 + [2 * 16 * 8]
    scratch = [pltpu.VMEM((n, FREQ), F32) for n in rows]
    params = pltpu.CompilerParams(vmem_limit_bytes=32 * 1024 * 1024)
    cost = pl.CostEstimate(flops=3_000_000, bytes_accessed=3_000_000, transcendentals=0)
    edge = pl.pallas_call(
        edge_kernel,
        out_shape=float_shape(64),
        in_specs=[smem] + [vmem] * (2 + len(shared)),
        scratch_shapes=scratch,
        compiler_params=params,
        cost_estimate=cost,
    )(starts, came_even, even, *shared)
    return pl.pallas_call(
        last_kernel,
        out_shape=float_shape(8 * 2 * DIST * 2),
        in_specs=[smem] + [vmem] * (4 + len(shared)),
        out_specs=pl.BlockSpec(memory_space=pltpu.HBM),
        scratch_shapes=[pltpu.VMEM((64, FREQ), F32)] + scratch + [pltpu.SemaphoreType.DMA((3,))],
        compiler_params=params,
        cost_estimate=cost,
    )(starts, came_odd, odd, *shared, mid, edge)


def on_device(frames, disk_mask, offsets, filter_gain, filter_mix):
    packed = pack(frames, disk_mask).reshape(TILES, LOCAL, WIDE * ROWS)
    received = lax.all_to_all(packed, "tile", split_axis=0, concat_axis=0, tiled=True)
    series = received.reshape(FRAMES, WIDE * ROWS)
    own, even, odd = spectra(series, dft_table())
    starts = ((offsets[..., 1] + 4) * REACH + offsets[..., 0] + 4).reshape(DIST * OFFS)
    gain = filter_gain.reshape(1, FREQ)
    mix = filter_mix.reshape(1, FREQ)
    out = edges(starts, even, odd, middle(starts, own, disk_mask, gain, mix))
    return out.reshape(8, 2, DIST, 2, FREQ)


def solution(mesh):
    return jax.shard_map(
        on_device,
        mesh=mesh,
        in_specs=(P("tile", "band", None), P("band", None), P(), P(), P()),
        out_specs=P("band", "tile", None, None, None),
        check_vma=False,
    )
```

```python
import math

import jax
import jax.numpy as jnp
import numpy as np
from jax import lax
from jax.experimental import pallas as pl
from jax.experimental.pallas import tpu as pltpu
from jax.sharding import PartitionSpec as P

FRAMES = 512
FREQ = 128
DIST = 8
OFFS = 8
FLO = 48
TILES = 64
LOCAL = 8
ROWS = 32
COLS = 8
WIDE = 20
LEAD = 6
BLOCKS = 72
TALL = 48
REACH = 40
SIDE = 16

F32 = jnp.float32
BF16 = jnp.bfloat16


def dft_table():
    times = np.arange(FRAMES, dtype=np.int32)
    freqs = FLO + np.arange(FREQ, dtype=np.int32)
    phases = times[:, None] * freqs[None, :] % FRAMES
    angles = phases.astype(np.float32) * np.float32(2.0 * math.pi / FRAMES)
    factor = np.float32(1.0 / math.sqrt(FRAMES))
    both = np.concatenate([np.cos(angles) * factor, -np.sin(angles) * factor], axis=1)
    return jnp.asarray(both.astype(np.float32)).astype(BF16)


def pack_kernel(
    frames_ref, mask_ref, out_ref, frames_vmem, mask_vmem, pick_ref, low_ref, high_ref, laid_ref, sems
):
    copies = [
        pltpu.make_async_copy(mask_ref, mask_vmem, sems.at[0]),
        pltpu.make_async_copy(frames_ref, frames_vmem, sems.at[1]),
    ]
    for copy in copies:
        copy.start()
    width = mask_vmem.shape[1]
    cols = lax.broadcasted_iota(jnp.int32, (BLOCKS, width), 1)
    block = lax.broadcasted_iota(jnp.int32, (BLOCKS, width), 0)
    place = cols - 8 * block + LEAD
    for c in range(COLS):
        pick_ref[c * BLOCKS : (c + 1) * BLOCKS, :] = jnp.where(place == c, 1.0, 0.0)
    for copy in copies:
        copy.wait()
    mask = mask_vmem[...].astype(F32)
    masked = (frames_vmem[...].astype(F32) * mask[None]).astype(BF16)
    turned = lax.dot_general(
        pick_ref[...].astype(BF16),
        masked.reshape(LOCAL * ROWS, width),
        (((1,), (1,)), ((), ())),
        preferred_element_type=F32,
    )
    lane_group = lax.broadcasted_iota(jnp.int32, (BLOCKS, 128), 1) // 32
    for half in range(2):
        lanes = slice(half * 128, half * 128 + 128)
        rolled = []
        for c in range(COLS):
            piece = turned[c * BLOCKS : (c + 1) * BLOCKS, lanes]
            rolled.append([piece if n == 0 else pltpu.roll(piece, 32 * n, 1) for n in range(4)])
        for f in range(4):
            for part in range(2):
                value = None
                for g in range(4):
                    piece = rolled[part * 4 + g][(g - f) % 4]
                    value = piece if value is None else jnp.where(lane_group == g, piece, value)
                at = half * 4 + f
                (low_ref, high_ref)[part][pl.ds(at, BLOCKS, stride=LOCAL), :] = value
    rows = TILES * LOCAL // 4
    parts = []
    for n in range(4):
        here = slice(n * rows, (n + 1) * rows)
        for at, source, start in (
            (0, low_ref, 0),
            (128, high_ref, 0),
            (256, low_ref, 8),
            (384, high_ref, 8),
            (512, low_ref, 16),
        ):
            start = start + n * rows
            laid_ref[here, at : at + 128] = source[start : start + rows, :].astype(BF16)
        parts.append(pltpu.make_async_copy(laid_ref.at[here], out_ref.at[here], sems.at[2 + n]))
        parts[n].start()
    for part in parts:
        part.wait()


def pack(frames, mask):
    return pl.pallas_call(
        pack_kernel,
        out_shape=jax.ShapeDtypeStruct((TILES * LOCAL, WIDE * ROWS), BF16),
        in_specs=[pl.BlockSpec(memory_space=pltpu.HBM)] * 2,
        out_specs=pl.BlockSpec(memory_space=pltpu.HBM),
        scratch_shapes=[
            pltpu.VMEM(frames.shape, BF16),
            pltpu.VMEM(mask.shape, jnp.int32),
            pltpu.VMEM((COLS * BLOCKS, mask.shape[1]), F32),
            pltpu.VMEM((BLOCKS * LOCAL, 128), F32),
            pltpu.VMEM((BLOCKS * LOCAL, 128), F32),
            pltpu.VMEM((TILES * LOCAL, WIDE * ROWS), BF16),
            pltpu.SemaphoreType.DMA((6,)),
        ],
        compiler_params=pltpu.CompilerParams(vmem_limit_bytes=60000000),
    )(frames, mask)


def spectra_kernel(series_ref, table_ref, pair_ref, own_ref, even_ref, odd_ref):
    spectrum = lax.dot_general(
        series_ref[...],
        table_ref[...],
        (((0,), (0,)), ((), ())),
        preferred_element_type=F32,
    )
    own_ref[...] = spectrum.astype(BF16)
    by_column = spectrum.reshape(WIDE, ROWS, 2 * FREQ)
    last = by_column[:, ROWS - 8 :].reshape(WIDE * 8, 2 * FREQ).astype(BF16)
    first = by_column[:, :8].reshape(WIDE * 8, 2 * FREQ).astype(BF16)
    odd_band = lax.axis_index("band") % 2

    @pl.when(odd_band == 0)
    def _():
        even_ref[...] = last
        odd_ref[...] = first

    @pl.when(odd_band == 1)
    def _():
        even_ref[...] = first
        odd_ref[...] = last


def spectra(series, table, pair):
    edge = jax.ShapeDtypeStruct((WIDE * 8, 2 * FREQ), BF16)
    return pl.pallas_call(
        spectra_kernel,
        out_shape=(jax.ShapeDtypeStruct((WIDE * ROWS, 2 * FREQ), BF16), edge, edge),
        compiler_params=pltpu.CompilerParams(vmem_limit_bytes=32 * 1024 * 1024),
    )(series, table, pair)


def select_kernel(offsets_ref, mask_ref, gain_ref, mix_ref, pick_ref, weight_ref, share_ref, pair_ref):
    shape = (COLS * 8, SIDE * 16)
    pixel = lax.broadcasted_iota(jnp.int32, shape, 0)
    lane = lax.broadcasted_iota(jnp.int32, shape, 1)
    apart = lane - (pixel // 8) * 16 - pixel % 8

    def distance(d, carry):
        total = jnp.zeros(shape, F32)
        for k in range(OFFS):
            total = total + jnp.where(apart == offsets_ref[d * OFFS + k], 1.0, 0.0)
        picked = total.astype(BF16)
        at = pl.multiple_of(d * COLS * 8, COLS * 8)
        pick_ref[pl.ds(at, COLS * 8), 0 : SIDE * 16] = picked
        pick_ref[pl.ds(at, COLS * 8), SIDE * 16 : 2 * SIDE * 16] = picked
        return carry

    lax.fori_loop(0, DIST, distance, 0)
    tile = lax.axis_index("tile")
    wide = pl.multiple_of((tile // 16) * 128, 128)
    near = mask_ref[:, pl.ds(wide, 128)].astype(F32)
    near = pltpu.roll(near, (128 - 8 * (tile % 16)) % 128, 1)
    for part in range(2):
        total = jnp.zeros((ROWS, 128), F32)
        for c in range(part * 4, part * 4 + 4):
            weight = jnp.broadcast_to(near[:, c : c + 1], (ROWS, 128))
            total = total + weight
            for group in range(4):
                at = (group * COLS + c) * 8
                weight_ref[at : at + 8, :] = weight[group * 8 : group * 8 + 8]
        for block in range(8):
            count = total[block * 4 : block * 4 + 1]
            for k in range(1, 4):
                count = count + total[block * 4 + k : block * 4 + k + 1]
            share_ref[block * 2 + part : block * 2 + part + 1, :] = 1.0 / jnp.maximum(count, 1.0)
    pair_ref[0:1, :] = gain_ref[...]
    pair_ref[1:2, :] = mix_ref[...]


def filtered(tall, rim, at, rows, gain, mix):
    inner = tall[at : at + rows, :]
    beside = 0.25 * (
        tall[at + 1 : at + 1 + rows, :]
        + tall[at - 1 : at - 1 + rows, :]
        + tall[at + rim : at + rim + rows, :]
        + tall[at - rim : at - rim + rows, :]
    )
    return gain * inner + mix * (beside - inner)


def group_blocks(group, pick_ref, filt_re, filt_im, weight_ref, share_ref, out_ref, first, scratch):
    window, annulus, sums = scratch
    size = SIDE * 16
    for q in range(SIDE):
        at = q * REACH + group * 8
        for filt, lanes in ((filt_re, slice(0, FREQ)), (filt_im, slice(FREQ, 2 * FREQ))):
            value = filt[at : at + 16, :]
            high = value.astype(BF16)
            low = (value - high.astype(F32)).astype(BF16)
            window[q * 16 : q * 16 + 16, lanes] = high
            window[size + q * 16 : size + q * 16 + 16, lanes] = low
    annulus[...] = jnp.dot(pick_ref[...], window[...], preferred_element_type=F32)
    for part in range(2):
        centre = []
        for c in range(part * 4, part * 4 + 4):
            at = (c + 4) * REACH + 4 + group * 8
            weight = weight_ref[(group * COLS + c) * 8 : (group * COLS + c) * 8 + 8, :]
            centre.append((filt_re[at : at + 8, :] * weight, filt_im[at : at + 8, :] * weight))
        for d in range(DIST):
            first_sum = None
            for c in range(4):
                at = (d * COLS + part * 4 + c) * 8
                real_a = annulus[at : at + 8, :FREQ]
                imag_a = annulus[at : at + 8, FREQ:]
                real_c, imag_c = centre[c]
                one = real_c * real_a + imag_c * imag_a
                two = real_c * imag_a - imag_c * real_a
                first_sum = one if first_sum is None else first_sum + one
                second_sum = two if c == 0 else second_sum + two
            at = (part * 16 + 2 * d) * 8
            sums[at : at + 8, :] = first_sum
            sums[at + 8 : at + 16, :] = second_sum
    for half in range(2):
        for part in range(2):
            block = (group * 2 + half) * 2 + part
            share = jnp.broadcast_to(share_ref[block : block + 1, :], (8, 128))
            for piece in range(2):
                base = (part * 16 + piece * 8) * 8 + half * 4
                total = sums[pl.ds(base, 8, stride=8), :]
                for k in range(1, 4):
                    total = total + sums[pl.ds(base + k, 8, stride=8), :]
                to = first + (half * 2 + part) * 16 + piece * 8
                out_ref[to : to + 8, :] = total * share


def middle_kernel(
    own_ref, pick_ref, weight_ref, share_ref, pair_ref, out_ref, filt_re, filt_im, own_re, own_im, *scratch
):
    own_re[...] = own_ref[:, :FREQ].astype(F32)
    own_im[...] = own_ref[:, FREQ:].astype(F32)
    gain = pair_ref[0:1, :]
    mix = pair_ref[1:2, :]
    for source, filt in ((own_re, filt_re), (own_im, filt_im)):
        for q in range(SIDE):
            value = filtered(source, ROWS, (q + 2) * ROWS + 1, ROWS - 2, gain, mix)
            filt[q * REACH + 5 : q * REACH + 5 + ROWS - 2, :] = value
    for n in range(2):
        group_blocks(
            1 + n, pick_ref, filt_re, filt_im, weight_ref, share_ref, out_ref, n * 64, scratch
        )


def outer_kernel(
    came_even,
    came_odd,
    went_even,
    went_odd,
    pick_ref,
    weight_ref,
    share_ref,
    pair_ref,
    mid_ref,
    own_filt_re,
    own_filt_im,
    out_ref,
    tall_re,
    tall_im,
    filt_re,
    filt_im,
    result,
    sems,
    *scratch,
):
    copies = [
        pltpu.make_async_copy(mid_ref, out_ref.at[64:192], sems.at[0]),
        pltpu.make_async_copy(result.at[0:64], out_ref.at[0:64], sems.at[1]),
        pltpu.make_async_copy(result.at[64:128], out_ref.at[192:256], sems.at[2]),
    ]
    copies[0].start()
    odd = lax.axis_index("band") % 2
    half = WIDE * 16
    for ref, at in (
        (came_even, (1 - odd) * (half + 8)),
        (went_even, odd * 8 + (1 - odd) * half),
        (came_odd, odd * (half + 8)),
        (went_odd, odd * half + (1 - odd) * 8),
    ):
        value = ref[...].astype(F32).reshape(WIDE, 8, 2 * FREQ)
        at = pl.multiple_of(at, 8)
        for q in range(WIDE):
            tall_re[pl.ds(at + q * 16, 8), :] = value[q, :, :FREQ]
            tall_im[pl.ds(at + q * 16, 8), :] = value[q, :, FREQ:]
    gain = pair_ref[0:1, :]
    mix = pair_ref[1:2, :]
    for n, group in enumerate((0, 3)):
        edge, kept = ((0, 8), (32, 24))[n]
        for tall, inside, filt in (
            (tall_re, own_filt_re, filt_re),
            (tall_im, own_filt_im, filt_im),
        ):
            for q in range(SIDE):
                at = q * REACH
                value = filtered(tall, 16, n * half + (q + 2) * 16 + 4, 8, gain, mix)
                filt[at + edge : at + edge + 8, :] = value
                filt[at + kept : at + kept + 8, :] = inside[at + kept : at + kept + 8, :]
        group_blocks(
            group, pick_ref, filt_re, filt_im, weight_ref, share_ref, result, n * 64, scratch
        )
        copies[1 + n].start()
    for copy in copies:
        copy.wait()


def float_shape(rows):
    return jax.ShapeDtypeStruct((rows, FREQ), F32)


VMEM = pl.BlockSpec(memory_space=pltpu.VMEM)
SMEM = pl.BlockSpec(memory_space=pltpu.SMEM)
GROUP_SCRATCH = [
    pltpu.VMEM((2 * SIDE * 16, 2 * FREQ), BF16),
    pltpu.VMEM((DIST * COLS * 8, 2 * FREQ), F32),
    pltpu.VMEM((2 * 16 * 8, FREQ), F32),
]


def params():
    return pltpu.CompilerParams(vmem_limit_bytes=32 * 1024 * 1024)


def select(steps, mask, gain, mix):
    return pl.pallas_call(
        select_kernel,
        out_shape=(
            jax.ShapeDtypeStruct((DIST * COLS * 8, 2 * SIDE * 16), BF16),
            float_shape(COLS * ROWS),
            float_shape(16),
            float_shape(8),
        ),
        in_specs=[SMEM] + [VMEM] * 3,
        compiler_params=params(),
        cost_estimate=pl.CostEstimate(flops=4_000_000, bytes_accessed=4_000_000, transcendentals=0),
    )(steps, mask, gain, mix)


def middle(own, chosen):
    return pl.pallas_call(
        middle_kernel,
        out_shape=(float_shape(128), float_shape(SIDE * REACH), float_shape(SIDE * REACH)),
        in_specs=[VMEM] * 5,
        scratch_shapes=[pltpu.VMEM((WIDE * ROWS, FREQ), F32)] * 2 + GROUP_SCRATCH,
        compiler_params=params(),
        cost_estimate=pl.CostEstimate(flops=6_000_000, bytes_accessed=4_000_000, transcendentals=0),
    )(own, *chosen)


def outer(even, odd, chosen, kept):
    bands = lax.axis_size("band")
    pairs = [(i, i ^ 1) for i in range(bands)]
    between = [(i, ((i + 1) ^ 1) - 1) for i in range(1, bands - 1)]
    came_even = lax.ppermute(even, "band", pairs)
    came_odd = lax.ppermute(odd, "band", between)
    rows = [WIDE * 32] * 2 + [SIDE * REACH] * 2 + [128]
    return pl.pallas_call(
        outer_kernel,
        out_shape=float_shape(8 * 2 * DIST * 2),
        in_specs=[VMEM] * 11,
        out_specs=pl.BlockSpec(memory_space=pltpu.HBM),
        scratch_shapes=[pltpu.VMEM((n, FREQ), F32) for n in rows]
        + [pltpu.SemaphoreType.DMA((3,))]
        + GROUP_SCRATCH,
        compiler_params=params(),
    )(came_even, came_odd, even, odd, *chosen, *kept)


def on_device(frames, disk_mask, offsets, filter_gain, filter_mix):
    packed = pack(frames, disk_mask).reshape(TILES, LOCAL, WIDE * ROWS)
    received = lax.all_to_all(packed, "tile", split_axis=0, concat_axis=0, tiled=True)
    steps = ((offsets[..., 1] + 4) * 16 + offsets[..., 0] + 4).reshape(DIST * OFFS)
    gain = filter_gain.reshape(1, FREQ)
    mix = filter_mix.reshape(1, FREQ)
    chosen = select(steps, disk_mask, gain, mix)
    series = received.reshape(FRAMES, WIDE * ROWS)
    own, even, odd = spectra(series, dft_table(), chosen[-1])
    out = outer(even, odd, chosen, middle(own, chosen))
    return out.reshape(8, 2, DIST, 2, FREQ)


def solution(mesh):
    return jax.shard_map(
        on_device,
        mesh=mesh,
        in_specs=(P("tile", "band", None), P("band", None), P(), P(), P()),
        out_specs=P("band", "tile", None, None, None),
        check_vma=False,
    )
```

```python
import math

import jax
import jax.numpy as jnp
import numpy as np
from jax import lax
from jax.experimental import pallas as pl
from jax.experimental.pallas import tpu as pltpu
from jax.sharding import PartitionSpec as P

FRAMES = 512
FREQ = 128
DIST = 8
OFFS = 8
FLO = 48
TILES = 64
LOCAL = 8
ROWS = 32
COLS = 8
WIDE = 20
LEAD = 6
BLOCKS = 72
TALL = 48
REACH = 40
SIDE = 16

F32 = jnp.float32
BF16 = jnp.bfloat16


def dft_table():
    times = np.arange(FRAMES, dtype=np.int32)
    freqs = FLO + np.arange(FREQ, dtype=np.int32)
    phases = times[:, None] * freqs[None, :] % FRAMES
    angles = phases.astype(np.float32) * np.float32(2.0 * math.pi / FRAMES)
    factor = np.float32(1.0 / math.sqrt(FRAMES))
    both = np.concatenate([np.cos(angles) * factor, -np.sin(angles) * factor], axis=1)
    return jnp.asarray(both.astype(np.float32)).astype(BF16)


def pack_kernel(
    frames_ref, mask_ref, out_ref, frames_vmem, mask_vmem, pick_ref, low_ref, high_ref, laid_ref, sems
):
    copies = [
        pltpu.make_async_copy(mask_ref, mask_vmem, sems.at[0]),
        pltpu.make_async_copy(frames_ref, frames_vmem, sems.at[1]),
    ]
    for copy in copies:
        copy.start()
    width = mask_vmem.shape[1]
    cols = lax.broadcasted_iota(jnp.int32, (BLOCKS, width), 1)
    block = lax.broadcasted_iota(jnp.int32, (BLOCKS, width), 0)
    place = cols - 8 * block + LEAD
    for c in range(COLS):
        pick_ref[c * BLOCKS : (c + 1) * BLOCKS, :] = jnp.where(place == c, 1.0, 0.0)
    for copy in copies:
        copy.wait()
    mask = mask_vmem[...].astype(F32)
    masked = (frames_vmem[...].astype(F32) * mask[None]).astype(BF16)
    turned = lax.dot_general(
        pick_ref[...].astype(BF16),
        masked.reshape(LOCAL * ROWS, width),
        (((1,), (1,)), ((), ())),
        preferred_element_type=F32,
    )
    lane_group = lax.broadcasted_iota(jnp.int32, (BLOCKS, 128), 1) // 32
    for half in range(2):
        lanes = slice(half * 128, half * 128 + 128)
        rolled = []
        for c in range(COLS):
            piece = turned[c * BLOCKS : (c + 1) * BLOCKS, lanes]
            rolled.append([piece if n == 0 else pltpu.roll(piece, 32 * n, 1) for n in range(4)])
        for f in range(4):
            for part in range(2):
                value = None
                for g in range(4):
                    piece = rolled[part * 4 + g][(g - f) % 4]
                    value = piece if value is None else jnp.where(lane_group == g, piece, value)
                at = half * 4 + f
                (low_ref, high_ref)[part][pl.ds(at, BLOCKS, stride=LOCAL), :] = value
    rows = TILES * LOCAL // 4
    parts = []
    for n in range(4):
        here = slice(n * rows, (n + 1) * rows)
        for at, source, start in (
            (0, low_ref, 0),
            (128, high_ref, 0),
            (256, low_ref, 8),
            (384, high_ref, 8),
            (512, low_ref, 16),
        ):
            start = start + n * rows
            laid_ref[here, at : at + 128] = source[start : start + rows, :].astype(BF16)
        parts.append(pltpu.make_async_copy(laid_ref.at[here], out_ref.at[here], sems.at[2 + n]))
        parts[n].start()
    for part in parts:
        part.wait()


def pack(frames, mask):
    return pl.pallas_call(
        pack_kernel,
        out_shape=jax.ShapeDtypeStruct((TILES * LOCAL, WIDE * ROWS), BF16),
        in_specs=[pl.BlockSpec(memory_space=pltpu.HBM)] * 2,
        out_specs=pl.BlockSpec(memory_space=pltpu.HBM),
        scratch_shapes=[
            pltpu.VMEM(frames.shape, BF16),
            pltpu.VMEM(mask.shape, jnp.int32),
            pltpu.VMEM((COLS * BLOCKS, mask.shape[1]), F32),
            pltpu.VMEM((BLOCKS * LOCAL, 128), F32),
            pltpu.VMEM((BLOCKS * LOCAL, 128), F32),
            pltpu.VMEM((TILES * LOCAL, WIDE * ROWS), BF16),
            pltpu.SemaphoreType.DMA((6,)),
        ],
        compiler_params=pltpu.CompilerParams(vmem_limit_bytes=60000000),
    )(frames, mask)


def spectra_kernel(series_ref, table_ref, pair_ref, own_ref, first_ref, last_ref):
    spectrum = lax.dot_general(
        series_ref[...],
        table_ref[...],
        (((0,), (0,)), ((), ())),
        preferred_element_type=F32,
    )
    own_ref[...] = spectrum.astype(BF16)
    by_column = spectrum.reshape(WIDE, ROWS, 2 * FREQ)
    first_ref[...] = by_column[:, :8].reshape(WIDE * 8, 2 * FREQ).astype(BF16)
    last_ref[...] = by_column[:, ROWS - 8 :].reshape(WIDE * 8, 2 * FREQ).astype(BF16)


def spectra(series, table, pair):
    edge = jax.ShapeDtypeStruct((WIDE * 8, 2 * FREQ), BF16)
    return pl.pallas_call(
        spectra_kernel,
        out_shape=(jax.ShapeDtypeStruct((WIDE * ROWS, 2 * FREQ), BF16), edge, edge),
        compiler_params=pltpu.CompilerParams(vmem_limit_bytes=32 * 1024 * 1024),
    )(series, table, pair)


def select_kernel(offsets_ref, mask_ref, gain_ref, mix_ref, pick_ref, weight_ref, share_ref, pair_ref):
    shape = (COLS * 8, SIDE * 16)
    pixel = lax.broadcasted_iota(jnp.int32, shape, 0)
    lane = lax.broadcasted_iota(jnp.int32, shape, 1)
    apart = lane - (pixel // 8) * 16 - pixel % 8

    def distance(d, carry):
        total = jnp.zeros(shape, F32)
        for k in range(OFFS):
            total = total + jnp.where(apart == offsets_ref[d * OFFS + k], 1.0, 0.0)
        picked = total.astype(BF16)
        at = pl.multiple_of(d * COLS * 8, COLS * 8)
        pick_ref[pl.ds(at, COLS * 8), 0 : SIDE * 16] = picked
        pick_ref[pl.ds(at, COLS * 8), SIDE * 16 : 2 * SIDE * 16] = picked
        return carry

    lax.fori_loop(0, DIST, distance, 0)
    tile = lax.axis_index("tile")
    wide = pl.multiple_of((tile // 16) * 128, 128)
    near = mask_ref[:, pl.ds(wide, 128)].astype(F32)
    near = pltpu.roll(near, (128 - 8 * (tile % 16)) % 128, 1)
    for part in range(2):
        total = jnp.zeros((ROWS, 128), F32)
        for c in range(part * 4, part * 4 + 4):
            weight = jnp.broadcast_to(near[:, c : c + 1], (ROWS, 128))
            total = total + weight
            for group in range(4):
                at = (group * COLS + c) * 8
                weight_ref[at : at + 8, :] = weight[group * 8 : group * 8 + 8]
        for block in range(8):
            count = total[block * 4 : block * 4 + 1]
            for k in range(1, 4):
                count = count + total[block * 4 + k : block * 4 + k + 1]
            share_ref[block * 2 + part : block * 2 + part + 1, :] = 1.0 / jnp.maximum(count, 1.0)
    pair_ref[0:1, :] = gain_ref[...]
    pair_ref[1:2, :] = mix_ref[...]


def filtered(tall, rim, at, rows, gain, mix):
    inner = tall[at : at + rows, :]
    beside = 0.25 * (
        tall[at + 1 : at + 1 + rows, :]
        + tall[at - 1 : at - 1 + rows, :]
        + tall[at + rim : at + rim + rows, :]
        + tall[at - rim : at - rim + rows, :]
    )
    return gain * inner + mix * (beside - inner)


def group_blocks(group, pick_ref, filt_re, filt_im, weight_ref, share_ref, out_ref, first, scratch):
    window, annulus, sums = scratch
    size = SIDE * 16
    for q in range(SIDE):
        at = q * REACH + group * 8
        for filt, lanes in ((filt_re, slice(0, FREQ)), (filt_im, slice(FREQ, 2 * FREQ))):
            value = filt[at : at + 16, :]
            high = value.astype(BF16)
            low = (value - high.astype(F32)).astype(BF16)
            window[q * 16 : q * 16 + 16, lanes] = high
            window[size + q * 16 : size + q * 16 + 16, lanes] = low
    annulus[...] = jnp.dot(pick_ref[...], window[...], preferred_element_type=F32)
    for part in range(2):
        centre = []
        for c in range(part * 4, part * 4 + 4):
            at = (c + 4) * REACH + 4 + group * 8
            weight = weight_ref[(group * COLS + c) * 8 : (group * COLS + c) * 8 + 8, :]
            centre.append((filt_re[at : at + 8, :] * weight, filt_im[at : at + 8, :] * weight))
        for d in range(DIST):
            first_sum = None
            for c in range(4):
                at = (d * COLS + part * 4 + c) * 8
                real_a = annulus[at : at + 8, :FREQ]
                imag_a = annulus[at : at + 8, FREQ:]
                real_c, imag_c = centre[c]
                one = real_c * real_a + imag_c * imag_a
                two = real_c * imag_a - imag_c * real_a
                first_sum = one if first_sum is None else first_sum + one
                second_sum = two if c == 0 else second_sum + two
            at = (part * 16 + 2 * d) * 8
            sums[at : at + 8, :] = first_sum
            sums[at + 8 : at + 16, :] = second_sum
    for half in range(2):
        for part in range(2):
            block = (group * 2 + half) * 2 + part
            share = jnp.broadcast_to(share_ref[block : block + 1, :], (8, 128))
            for piece in range(2):
                base = (part * 16 + piece * 8) * 8 + half * 4
                total = sums[pl.ds(base, 8, stride=8), :]
                for k in range(1, 4):
                    total = total + sums[pl.ds(base + k, 8, stride=8), :]
                to = first + (half * 2 + part) * 16 + piece * 8
                out_ref[to : to + 8, :] = total * share


def middle_kernel(
    own_ref, pick_ref, weight_ref, share_ref, pair_ref, out_ref, filt_re, filt_im, own_re, own_im, *scratch
):
    own_re[...] = own_ref[:, :FREQ].astype(F32)
    own_im[...] = own_ref[:, FREQ:].astype(F32)
    gain = pair_ref[0:1, :]
    mix = pair_ref[1:2, :]
    for source, filt in ((own_re, filt_re), (own_im, filt_im)):
        for q in range(SIDE):
            value = filtered(source, ROWS, (q + 2) * ROWS + 1, ROWS - 2, gain, mix)
            filt[q * REACH + 5 : q * REACH + 5 + ROWS - 2, :] = value
    for n in range(2):
        group_blocks(
            1 + n, pick_ref, filt_re, filt_im, weight_ref, share_ref, out_ref, n * 64, scratch
        )


def outer_kernel(
    after_ref,
    before_ref,
    first_ref,
    last_ref,
    pick_ref,
    weight_ref,
    share_ref,
    pair_ref,
    mid_ref,
    own_filt_re,
    own_filt_im,
    out_ref,
    tall_re,
    tall_im,
    filt_re,
    filt_im,
    result,
    sems,
    *scratch,
):
    copies = [
        pltpu.make_async_copy(mid_ref, out_ref.at[64:192], sems.at[0]),
        pltpu.make_async_copy(result.at[0:64], out_ref.at[0:64], sems.at[1]),
        pltpu.make_async_copy(result.at[64:128], out_ref.at[192:256], sems.at[2]),
    ]
    copies[0].start()
    half = WIDE * 16
    for ref, at in ((before_ref, 0), (first_ref, 8), (last_ref, half), (after_ref, half + 8)):
        value = ref[...].astype(F32).reshape(WIDE, 8, 2 * FREQ)
        for q in range(WIDE):
            tall_re[at + q * 16 : at + q * 16 + 8, :] = value[q, :, :FREQ]
            tall_im[at + q * 16 : at + q * 16 + 8, :] = value[q, :, FREQ:]
    gain = pair_ref[0:1, :]
    mix = pair_ref[1:2, :]
    for n, group in enumerate((0, 3)):
        edge, kept = ((0, 8), (32, 24))[n]
        for tall, inside, filt in (
            (tall_re, own_filt_re, filt_re),
            (tall_im, own_filt_im, filt_im),
        ):
            for q in range(SIDE):
                at = q * REACH
                value = filtered(tall, 16, n * half + (q + 2) * 16 + 4, 8, gain, mix)
                filt[at + edge : at + edge + 8, :] = value
                filt[at + kept : at + kept + 8, :] = inside[at + kept : at + kept + 8, :]
        group_blocks(
            group, pick_ref, filt_re, filt_im, weight_ref, share_ref, result, n * 64, scratch
        )
        copies[1 + n].start()
    for copy in copies:
        copy.wait()


def float_shape(rows):
    return jax.ShapeDtypeStruct((rows, FREQ), F32)


VMEM = pl.BlockSpec(memory_space=pltpu.VMEM)
SMEM = pl.BlockSpec(memory_space=pltpu.SMEM)
GROUP_SCRATCH = [
    pltpu.VMEM((2 * SIDE * 16, 2 * FREQ), BF16),
    pltpu.VMEM((DIST * COLS * 8, 2 * FREQ), F32),
    pltpu.VMEM((2 * 16 * 8, FREQ), F32),
]


def params():
    return pltpu.CompilerParams(vmem_limit_bytes=32 * 1024 * 1024)


def select(steps, mask, gain, mix):
    return pl.pallas_call(
        select_kernel,
        out_shape=(
            jax.ShapeDtypeStruct((DIST * COLS * 8, 2 * SIDE * 16), BF16),
            float_shape(COLS * ROWS),
            float_shape(16),
            float_shape(8),
        ),
        in_specs=[SMEM] + [VMEM] * 3,
        compiler_params=params(),
        cost_estimate=pl.CostEstimate(flops=4_000_000, bytes_accessed=4_000_000, transcendentals=0),
    )(steps, mask, gain, mix)


def middle(own, chosen):
    return pl.pallas_call(
        middle_kernel,
        out_shape=(float_shape(128), float_shape(SIDE * REACH), float_shape(SIDE * REACH)),
        in_specs=[VMEM] * 5,
        scratch_shapes=[pltpu.VMEM((WIDE * ROWS, FREQ), F32)] * 2 + GROUP_SCRATCH,
        compiler_params=params(),
        cost_estimate=pl.CostEstimate(flops=6_000_000, bytes_accessed=4_000_000, transcendentals=0),
    )(own, *chosen)


def outer(first, last, chosen, kept):
    bands = lax.axis_size("band")
    up = [(i, i + 1) for i in range(bands - 1)]
    down = [(j, i) for i, j in up]
    after = lax.ppermute(first, "band", down)
    before = lax.ppermute(last, "band", up)
    rows = [WIDE * 32] * 2 + [SIDE * REACH] * 2 + [128]
    return pl.pallas_call(
        outer_kernel,
        out_shape=float_shape(8 * 2 * DIST * 2),
        in_specs=[VMEM] * 11,
        out_specs=pl.BlockSpec(memory_space=pltpu.HBM),
        scratch_shapes=[pltpu.VMEM((n, FREQ), F32) for n in rows]
        + [pltpu.SemaphoreType.DMA((3,))]
        + GROUP_SCRATCH,
        compiler_params=params(),
    )(after, before, first, last, *chosen, *kept)


def on_device(frames, disk_mask, offsets, filter_gain, filter_mix):
    packed = pack(frames, disk_mask).reshape(TILES, LOCAL, WIDE * ROWS)
    received = lax.all_to_all(packed, "tile", split_axis=0, concat_axis=0, tiled=True)
    steps = ((offsets[..., 1] + 4) * 16 + offsets[..., 0] + 4).reshape(DIST * OFFS)
    gain = filter_gain.reshape(1, FREQ)
    mix = filter_mix.reshape(1, FREQ)
    chosen = select(steps, disk_mask, gain, mix)
    series = received.reshape(FRAMES, WIDE * ROWS)
    own, first, last = spectra(series, dft_table(), chosen[-1])
    out = outer(first, last, chosen, middle(own, chosen))
    return out.reshape(8, 2, DIST, 2, FREQ)


def solution(mesh):
    return jax.shard_map(
        on_device,
        mesh=mesh,
        in_specs=(P("tile", "band", None), P("band", None), P(), P(), P()),
        out_specs=P("band", "tile", None, None, None),
        check_vma=False,
    )
```

```python
import math

import jax
import jax.numpy as jnp
import numpy as np
from jax import lax
from jax.experimental import pallas as pl
from jax.experimental.pallas import tpu as pltpu
from jax.sharding import PartitionSpec as P

FRAMES = 512
FREQ = 128
DIST = 8
OFFS = 8
FLO = 48
CHIPS = 32
LOCAL = 8
ROWS = 32
COLS = 8
WIDE = 20
SPAN = 28
LEAD = 6
BLOCKS = 72
TALL = 48
REACH = 40
SIDE = 16

F32 = jnp.float32
BF16 = jnp.bfloat16


def dft_table():
    times = np.arange(FRAMES, dtype=np.int32).reshape(CHIPS, 2, LOCAL)
    times = times.transpose(1, 0, 2).reshape(FRAMES)
    freqs = FLO + np.arange(FREQ, dtype=np.int32)
    phases = times[:, None] * freqs[None, :] % FRAMES
    angles = phases.astype(np.float32) * np.float32(2.0 * math.pi / FRAMES)
    factor = np.float32(1.0 / math.sqrt(FRAMES))
    both = np.concatenate([np.cos(angles) * factor, -np.sin(angles) * factor], axis=1)
    return jnp.asarray(both.astype(np.float32)).astype(BF16)


def exchanged(values, groups, distance):
    upper = (groups // distance) % 2 == 1
    result = list(values)
    for n in range(4):
        if (n // distance) % 2 == 0:
            m = n + distance
            result[n] = jnp.where(upper, pltpu.roll(values[m], 32 * distance, 1), values[n])
            result[m] = jnp.where(upper, values[m], pltpu.roll(values[n], 128 - 32 * distance, 1))
    return result


def pack_kernel(
    frames_ref, mask_ref, out_ref, frames_vmem, mask_vmem, pick_ref, low_ref, high_ref, laid_ref, sems
):
    copies = [
        pltpu.make_async_copy(mask_ref, mask_vmem, sems.at[0]),
        pltpu.make_async_copy(frames_ref, frames_vmem, sems.at[1]),
    ]
    for copy in copies:
        copy.start()
    width = mask_vmem.shape[1]
    cols = lax.broadcasted_iota(jnp.int32, (BLOCKS, width), 1)
    block = lax.broadcasted_iota(jnp.int32, (BLOCKS, width), 0)
    place = cols - 8 * block + LEAD
    for c in range(COLS):
        pick_ref[c * BLOCKS : (c + 1) * BLOCKS, :] = jnp.where(place == c, 1.0, 0.0)
    for copy in copies:
        copy.wait()
    mask = mask_vmem[...].astype(F32)
    masked = (frames_vmem[...].astype(F32) * mask[None]).astype(BF16)
    turned = lax.dot_general(
        pick_ref[...].astype(BF16),
        masked.reshape(LOCAL * ROWS, width),
        (((1,), (1,)), ((), ())),
        preferred_element_type=F32,
    )
    groups = lax.broadcasted_iota(jnp.int32, (BLOCKS, 128), 1) // 32
    for part, ref in ((0, low_ref), (1, high_ref)):
        for half in range(2):
            lanes = slice(half * 128, half * 128 + 128)
            values = [
                turned[(part * 4 + g) * BLOCKS : (part * 4 + g + 1) * BLOCKS, lanes]
                for g in range(4)
            ]
            values = exchanged(exchanged(values, groups, 2), groups, 1)
            for f in range(4):
                ref[pl.ds(half * 4 + f, BLOCKS, stride=LOCAL), :] = values[f]
    for part, ref in ((0, low_ref), (1, high_ref)):
        laid = ref[...].reshape(BLOCKS // 2, 2, LOCAL, 128).astype(BF16)
        laid_ref[:, :, :, part * 128 : part * 128 + 128] = laid
    parts = [
        pltpu.make_async_copy(
            laid_ref.at[start : start + CHIPS, parity, :, 0:size],
            out_ref.at[:, :, at : at + size],
            sems.at[n],
        )
        for n, (start, parity, at, size) in enumerate(
            ((0, 0, 0, 256), (0, 1, 256, 256), (1, 0, 512, 256), (1, 1, 768, 128))
        )
    ]
    for part in parts:
        part.start()
    for part in parts:
        part.wait()


def pack(frames, mask):
    return pl.pallas_call(
        pack_kernel,
        out_shape=jax.ShapeDtypeStruct((CHIPS, LOCAL, SPAN * ROWS), BF16),
        in_specs=[pl.BlockSpec(memory_space=pltpu.HBM)] * 2,
        out_specs=pl.BlockSpec(memory_space=pltpu.HBM),
        scratch_shapes=[
            pltpu.VMEM(frames.shape, BF16),
            pltpu.VMEM(mask.shape, jnp.int32),
            pltpu.VMEM((COLS * BLOCKS, mask.shape[1]), F32),
            pltpu.VMEM((BLOCKS * LOCAL, 128), F32),
            pltpu.VMEM((BLOCKS * LOCAL, 128), F32),
            pltpu.VMEM((BLOCKS // 2, 2, LOCAL, 256), BF16),
            pltpu.SemaphoreType.DMA((4,)),
        ],
        compiler_params=pltpu.CompilerParams(vmem_limit_bytes=60000000),
    )(frames, mask)


def spectra_kernel(mine_ref, other_ref, table_ref, own_ref, first_ref, last_ref):
    core = lax.axis_index("tile") % 2
    count = FRAMES // 2
    lanes = pl.ds(pl.multiple_of(core * COLS * ROWS, 128), WIDE * ROWS)
    spectrum = None
    for ref, at in ((mine_ref, core), (other_ref, 1 - core)):
        part = lax.dot_general(
            ref[:, :, lanes].reshape(count, WIDE * ROWS),
            table_ref[pl.ds(pl.multiple_of(at * count, count), count), :],
            (((0,), (0,)), ((), ())),
            preferred_element_type=F32,
        )
        spectrum = part if spectrum is None else spectrum + part
    own_ref[...] = spectrum.astype(BF16)
    by_column = spectrum.reshape(WIDE, ROWS, 2 * FREQ)
    first_ref[...] = by_column[:, :8].reshape(WIDE * 8, 2 * FREQ).astype(BF16)
    last_ref[...] = by_column[:, ROWS - 8 :].reshape(WIDE * 8, 2 * FREQ).astype(BF16)


def spectra(mine, other, table):
    edge = jax.ShapeDtypeStruct((WIDE * 8, 2 * FREQ), BF16)
    return pl.pallas_call(
        spectra_kernel,
        out_shape=(jax.ShapeDtypeStruct((WIDE * ROWS, 2 * FREQ), BF16), edge, edge),
        compiler_params=pltpu.CompilerParams(vmem_limit_bytes=32 * 1024 * 1024),
    )(mine, other, table)


def select_kernel(offsets_ref, mask_ref, gain_ref, mix_ref, pick_ref, weight_ref, share_ref, pair_ref):
    shape = (COLS * 8, SIDE * 16)
    pixel = lax.broadcasted_iota(jnp.int32, shape, 0)
    lane = lax.broadcasted_iota(jnp.int32, shape, 1)
    apart = lane - (pixel // 8) * 16 - pixel % 8

    def distance(d, carry):
        total = jnp.zeros(shape, F32)
        for k in range(OFFS):
            total = total + jnp.where(apart == offsets_ref[d * OFFS + k], 1.0, 0.0)
        picked = total.astype(BF16)
        at = pl.multiple_of(d * COLS * 8, COLS * 8)
        pick_ref[pl.ds(at, COLS * 8), 0 : SIDE * 16] = picked
        pick_ref[pl.ds(at, COLS * 8), SIDE * 16 : 2 * SIDE * 16] = picked
        return carry

    lax.fori_loop(0, DIST, distance, 0)
    tile = lax.axis_index("tile")
    wide = pl.multiple_of((tile // 16) * 128, 128)
    near = mask_ref[:, pl.ds(wide, 128)].astype(F32)
    near = pltpu.roll(near, (128 - 8 * (tile % 16)) % 128, 1)
    for part in range(2):
        total = jnp.zeros((ROWS, 128), F32)
        for c in range(part * 4, part * 4 + 4):
            weight = jnp.broadcast_to(near[:, c : c + 1], (ROWS, 128))
            total = total + weight
            for group in range(4):
                at = (group * COLS + c) * 8
                weight_ref[at : at + 8, :] = weight[group * 8 : group * 8 + 8]
        for block in range(8):
            count = total[block * 4 : block * 4 + 1]
            for k in range(1, 4):
                count = count + total[block * 4 + k : block * 4 + k + 1]
            share_ref[block * 2 + part : block * 2 + part + 1, :] = 1.0 / jnp.maximum(count, 1.0)
    pair_ref[0:1, :] = gain_ref[...]
    pair_ref[1:2, :] = mix_ref[...]


def filtered(tall, rim, at, rows, gain, mix):
    inner = tall[at : at + rows, :]
    beside = 0.25 * (
        tall[at + 1 : at + 1 + rows, :]
        + tall[at - 1 : at - 1 + rows, :]
        + tall[at + rim : at + rim + rows, :]
        + tall[at - rim : at - rim + rows, :]
    )
    return gain * inner + mix * (beside - inner)


def group_blocks(group, pick_ref, filt_re, filt_im, weight_ref, share_ref, out_ref, first, scratch):
    window, annulus, sums = scratch
    size = SIDE * 16
    for q in range(SIDE):
        at = q * REACH + group * 8
        for filt, lanes in ((filt_re, slice(0, FREQ)), (filt_im, slice(FREQ, 2 * FREQ))):
            value = filt[at : at + 16, :]
            high = value.astype(BF16)
            low = (value - high.astype(F32)).astype(BF16)
            window[q * 16 : q * 16 + 16, lanes] = high
            window[size + q * 16 : size + q * 16 + 16, lanes] = low
    annulus[...] = jnp.dot(pick_ref[...], window[...], preferred_element_type=F32)
    for part in range(2):
        centre = []
        for c in range(part * 4, part * 4 + 4):
            at = (c + 4) * REACH + 4 + group * 8
            weight = weight_ref[(group * COLS + c) * 8 : (group * COLS + c) * 8 + 8, :]
            centre.append((filt_re[at : at + 8, :] * weight, filt_im[at : at + 8, :] * weight))
        for d in range(DIST):
            first_sum = None
            for c in range(4):
                at = (d * COLS + part * 4 + c) * 8
                real_a = annulus[at : at + 8, :FREQ]
                imag_a = annulus[at : at + 8, FREQ:]
                real_c, imag_c = centre[c]
                one = real_c * real_a + imag_c * imag_a
                two = real_c * imag_a - imag_c * real_a
                first_sum = one if first_sum is None else first_sum + one
                second_sum = two if c == 0 else second_sum + two
            at = (part * 16 + 2 * d) * 8
            sums[at : at + 8, :] = first_sum
            sums[at + 8 : at + 16, :] = second_sum
    for half in range(2):
        for part in range(2):
            block = (group * 2 + half) * 2 + part
            share = jnp.broadcast_to(share_ref[block : block + 1, :], (8, 128))
            for piece in range(2):
                base = (part * 16 + piece * 8) * 8 + half * 4
                total = sums[pl.ds(base, 8, stride=8), :]
                for k in range(1, 4):
                    total = total + sums[pl.ds(base + k, 8, stride=8), :]
                to = first + (half * 2 + part) * 16 + piece * 8
                out_ref[to : to + 8, :] = total * share


def middle_kernel(
    own_ref, pick_ref, weight_ref, share_ref, pair_ref, out_ref, filt_re, filt_im, own_re, own_im, *scratch
):
    own_re[...] = own_ref[:, :FREQ].astype(F32)
    own_im[...] = own_ref[:, FREQ:].astype(F32)
    gain = pair_ref[0:1, :]
    mix = pair_ref[1:2, :]
    for source, filt in ((own_re, filt_re), (own_im, filt_im)):
        for q in range(SIDE):
            value = filtered(source, ROWS, (q + 2) * ROWS + 1, ROWS - 2, gain, mix)
            filt[q * REACH + 5 : q * REACH + 5 + ROWS - 2, :] = value
    for n in range(2):
        group_blocks(
            1 + n, pick_ref, filt_re, filt_im, weight_ref, share_ref, out_ref, n * 64, scratch
        )


def outer_kernel(
    after_ref,
    before_ref,
    first_ref,
    last_ref,
    pick_ref,
    weight_ref,
    share_ref,
    pair_ref,
    mid_ref,
    own_filt_re,
    own_filt_im,
    out_ref,
    tall_re,
    tall_im,
    filt_re,
    filt_im,
    result,
    sems,
    *scratch,
):
    copies = [
        pltpu.make_async_copy(mid_ref, out_ref.at[64:192], sems.at[0]),
        pltpu.make_async_copy(result.at[0:64], out_ref.at[0:64], sems.at[1]),
        pltpu.make_async_copy(result.at[64:128], out_ref.at[192:256], sems.at[2]),
    ]
    copies[0].start()
    half = WIDE * 16
    for ref, at in ((before_ref, 0), (first_ref, 8), (last_ref, half), (after_ref, half + 8)):
        value = ref[...].astype(F32).reshape(WIDE, 8, 2 * FREQ)
        for q in range(WIDE):
            tall_re[at + q * 16 : at + q * 16 + 8, :] = value[q, :, :FREQ]
            tall_im[at + q * 16 : at + q * 16 + 8, :] = value[q, :, FREQ:]
    gain = pair_ref[0:1, :]
    mix = pair_ref[1:2, :]
    for n, group in enumerate((0, 3)):
        edge, kept = ((0, 8), (32, 24))[n]
        for tall, inside, filt in (
            (tall_re, own_filt_re, filt_re),
            (tall_im, own_filt_im, filt_im),
        ):
            for q in range(SIDE):
                at = q * REACH
                value = filtered(tall, 16, n * half + (q + 2) * 16 + 4, 8, gain, mix)
                filt[at + edge : at + edge + 8, :] = value
                filt[at + kept : at + kept + 8, :] = inside[at + kept : at + kept + 8, :]
        group_blocks(
            group, pick_ref, filt_re, filt_im, weight_ref, share_ref, result, n * 64, scratch
        )
        copies[1 + n].start()
    for copy in copies:
        copy.wait()


def float_shape(rows):
    return jax.ShapeDtypeStruct((rows, FREQ), F32)


VMEM = pl.BlockSpec(memory_space=pltpu.VMEM)
SMEM = pl.BlockSpec(memory_space=pltpu.SMEM)
GROUP_SCRATCH = [
    pltpu.VMEM((2 * SIDE * 16, 2 * FREQ), BF16),
    pltpu.VMEM((DIST * COLS * 8, 2 * FREQ), F32),
    pltpu.VMEM((2 * 16 * 8, FREQ), F32),
]


def params():
    return pltpu.CompilerParams(vmem_limit_bytes=32 * 1024 * 1024)


def select(steps, mask, gain, mix):
    return pl.pallas_call(
        select_kernel,
        out_shape=(
            jax.ShapeDtypeStruct((DIST * COLS * 8, 2 * SIDE * 16), BF16),
            float_shape(COLS * ROWS),
            float_shape(16),
            float_shape(8),
        ),
        in_specs=[SMEM] + [VMEM] * 3,
        compiler_params=params(),
        cost_estimate=pl.CostEstimate(flops=4_000_000, bytes_accessed=4_000_000, transcendentals=0),
    )(steps, mask, gain, mix)


def middle(own, chosen):
    return pl.pallas_call(
        middle_kernel,
        out_shape=(float_shape(128), float_shape(SIDE * REACH), float_shape(SIDE * REACH)),
        in_specs=[VMEM] * 5,
        scratch_shapes=[pltpu.VMEM((WIDE * ROWS, FREQ), F32)] * 2 + GROUP_SCRATCH,
        compiler_params=params(),
        cost_estimate=pl.CostEstimate(flops=6_000_000, bytes_accessed=4_000_000, transcendentals=0),
    )(own, *chosen)


def outer(first, last, chosen, kept):
    bands = lax.axis_size("band")
    up = [(i, i + 1) for i in range(bands - 1)]
    down = [(j, i) for i, j in up]
    after = lax.ppermute(first, "band", down)
    before = lax.ppermute(last, "band", up)
    rows = [WIDE * 32] * 2 + [SIDE * REACH] * 2 + [128]
    return pl.pallas_call(
        outer_kernel,
        out_shape=float_shape(8 * 2 * DIST * 2),
        in_specs=[VMEM] * 11,
        out_specs=pl.BlockSpec(memory_space=pltpu.HBM),
        scratch_shapes=[pltpu.VMEM((n, FREQ), F32) for n in rows]
        + [pltpu.SemaphoreType.DMA((3,))]
        + GROUP_SCRATCH,
        compiler_params=params(),
    )(after, before, first, last, *chosen, *kept)


def on_device(frames, disk_mask, offsets, filter_gain, filter_mix):
    same_core = [[2 * chip + core for chip in range(CHIPS)] for core in range(2)]
    mine = lax.all_to_all(
        pack(frames, disk_mask),
        "tile",
        split_axis=0,
        concat_axis=0,
        axis_index_groups=same_core,
        tiled=True,
    )
    steps = ((offsets[..., 1] + 4) * 16 + offsets[..., 0] + 4).reshape(DIST * OFFS)
    gain = filter_gain.reshape(1, FREQ)
    mix = filter_mix.reshape(1, FREQ)
    chosen = select(steps, disk_mask, gain, mix)
    mine, chosen = lax.optimization_barrier((mine, chosen))
    other = lax.ppermute(mine, "tile", [(i, i ^ 1) for i in range(2 * CHIPS)])
    own, first, last = spectra(mine, other, dft_table())
    out = outer(first, last, chosen, middle(own, chosen))
    return out.reshape(8, 2, DIST, 2, FREQ)


def solution(mesh):
    return jax.shard_map(
        on_device,
        mesh=mesh,
        in_specs=(P("tile", "band", None), P("band", None), P(), P(), P()),
        out_specs=P("band", "tile", None, None, None),
        check_vma=False,
    )
```

```python
import math

import jax
import jax.numpy as jnp
import numpy as np
from jax import lax
from jax.experimental import pallas as pl
from jax.experimental.pallas import tpu as pltpu
from jax.sharding import PartitionSpec as P

FRAMES = 512
FREQ = 128
DIST = 8
OFFS = 8
FLO = 48
CHIPS = 32
LOCAL = 8
ROWS = 32
COLS = 8
WIDE = 20
SPAN = 28
LEAD = 6
QUADS = (0, 16, 8, 24, 32, 48, 40)
BLOCKS = 72
TALL = 48
REACH = 40
SIDE = 16

F32 = jnp.float32
BF16 = jnp.bfloat16


def dft_table():
    times = np.arange(FRAMES, dtype=np.int32).reshape(CHIPS, 2, LOCAL)
    times = times.transpose(1, 0, 2).reshape(FRAMES)
    freqs = FLO + np.arange(FREQ, dtype=np.int32)
    phases = times[:, None] * freqs[None, :] % FRAMES
    angles = phases.astype(np.float32) * np.float32(2.0 * math.pi / FRAMES)
    factor = np.float32(1.0 / math.sqrt(FRAMES))
    both = np.concatenate([np.cos(angles) * factor, -np.sin(angles) * factor], axis=1)
    return jnp.asarray(both.astype(np.float32)).astype(BF16)


def exchanged(values, groups, distance):
    upper = (groups // distance) % 2 == 1
    result = list(values)
    for n in range(4):
        if (n // distance) % 2 == 0:
            m = n + distance
            result[n] = jnp.where(upper, pltpu.roll(values[m], 32 * distance, 1), values[n])
            result[m] = jnp.where(upper, values[m], pltpu.roll(values[n], 128 - 32 * distance, 1))
    return result


def pack_kernel(
    frames_ref, mask_ref, out_ref, frames_vmem, mask_vmem, pick_ref, low_ref, high_ref, sems
):
    copies = [
        pltpu.make_async_copy(mask_ref, mask_vmem, sems.at[0]),
        pltpu.make_async_copy(frames_ref, frames_vmem, sems.at[1]),
    ]
    for copy in copies:
        copy.start()
    width = mask_vmem.shape[1]
    cols = lax.broadcasted_iota(jnp.int32, (BLOCKS, width), 1)
    block = lax.broadcasted_iota(jnp.int32, (BLOCKS, width), 0)
    place = cols - 8 * block + LEAD
    for c in range(COLS):
        pick_ref[c * BLOCKS : (c + 1) * BLOCKS, :] = jnp.where(place == c, 1.0, 0.0)
    for copy in copies:
        copy.wait()
    mask = mask_vmem[...].astype(F32)
    masked = (frames_vmem[...].astype(F32) * mask[None]).astype(BF16)
    turned = lax.dot_general(
        pick_ref[...].astype(BF16),
        masked.reshape(LOCAL * ROWS, width),
        (((1,), (1,)), ((), ())),
        preferred_element_type=F32,
    )
    groups = lax.broadcasted_iota(jnp.int32, (BLOCKS, 128), 1) // 32
    for part, ref in ((0, low_ref), (1, high_ref)):
        for half in range(2):
            lanes = slice(half * 128, half * 128 + 128)
            values = [
                turned[(part * 4 + g) * BLOCKS : (part * 4 + g + 1) * BLOCKS, lanes]
                for g in range(4)
            ]
            values = exchanged(exchanged(values, groups, 2), groups, 1)
            for f in range(4):
                ref[pl.ds(half * 4 + f, BLOCKS, stride=LOCAL), :] = values[f]
    count = CHIPS * 16
    for at, ref, start in ((0, low_ref, 0), (16, high_ref, 0), (32, low_ref, 16)):
        laid = ref[start : start + count, :].reshape(CHIPS, 16, 128)
        out_ref[:, at : at + 16, :] = laid.astype(BF16)
    laid = high_ref[16 : 16 + count, :].reshape(CHIPS, 16, 128)
    out_ref[:, 48:56, :] = laid[:, 0:8, :].astype(BF16)


def pack(frames, mask):
    return pl.pallas_call(
        pack_kernel,
        out_shape=pltpu.VMEM((CHIPS, 2 * SPAN, 128), BF16),
        in_specs=[pl.BlockSpec(memory_space=pltpu.HBM)] * 2,
        scratch_shapes=[
            pltpu.VMEM(frames.shape, BF16),
            pltpu.VMEM(mask.shape, jnp.int32),
            pltpu.VMEM((COLS * BLOCKS, mask.shape[1]), F32),
            pltpu.VMEM((BLOCKS * LOCAL, 128), F32),
            pltpu.VMEM((BLOCKS * LOCAL, 128), F32),
            pltpu.SemaphoreType.DMA((2,)),
        ],
        compiler_params=pltpu.CompilerParams(vmem_limit_bytes=60000000),
    )(frames, mask)


def spectra_kernel(mine_ref, other_ref, table_ref, own_ref, first_ref, last_ref):
    core = lax.axis_index("tile") % 2
    count = FRAMES // 2
    spectrum = None
    for ref, at in ((mine_ref, core), (other_ref, 1 - core)):
        quads = [ref[:, row : row + 8, :].reshape(count, 128) for row in QUADS]
        series = [jnp.where(core == 0, quads[n], quads[n + 2]) for n in range(5)]
        part = lax.dot_general(
            jnp.concatenate(series, axis=1),
            table_ref[pl.ds(pl.multiple_of(at * count, count), count), :],
            (((0,), (0,)), ((), ())),
            preferred_element_type=F32,
        )
        spectrum = part if spectrum is None else spectrum + part
    own_ref[...] = spectrum.astype(BF16)
    by_column = spectrum.reshape(WIDE, ROWS, 2 * FREQ)
    first_ref[...] = by_column[:, :8].reshape(WIDE * 8, 2 * FREQ).astype(BF16)
    last_ref[...] = by_column[:, ROWS - 8 :].reshape(WIDE * 8, 2 * FREQ).astype(BF16)


def spectra(mine, other, table):
    edge = jax.ShapeDtypeStruct((WIDE * 8, 2 * FREQ), BF16)
    return pl.pallas_call(
        spectra_kernel,
        out_shape=(jax.ShapeDtypeStruct((WIDE * ROWS, 2 * FREQ), BF16), edge, edge),
        compiler_params=pltpu.CompilerParams(vmem_limit_bytes=32 * 1024 * 1024),
    )(mine, other, table)


def select_kernel(offsets_ref, mask_ref, pick_ref, weight_ref, share_ref):
    shape = (COLS * 8, SIDE * 16)
    pixel = lax.broadcasted_iota(jnp.int32, shape, 0)
    lane = lax.broadcasted_iota(jnp.int32, shape, 1)
    apart = lane - (pixel // 8) * 16 - pixel % 8

    def distance(d, carry):
        total = jnp.zeros(shape, F32)
        for k in range(OFFS):
            total = total + jnp.where(apart == offsets_ref[d * OFFS + k], 1.0, 0.0)
        picked = total.astype(BF16)
        at = pl.multiple_of(d * COLS * 8, COLS * 8)
        pick_ref[pl.ds(at, COLS * 8), 0 : SIDE * 16] = picked
        pick_ref[pl.ds(at, COLS * 8), SIDE * 16 : 2 * SIDE * 16] = picked
        return carry

    lax.fori_loop(0, DIST, distance, 0)
    tile = lax.axis_index("tile")
    wide = pl.multiple_of((tile // 16) * 128, 128)
    near = mask_ref[:, pl.ds(wide, 128)].astype(F32)
    near = pltpu.roll(near, (128 - 8 * (tile % 16)) % 128, 1)
    for part in range(2):
        total = jnp.zeros((ROWS, 128), F32)
        for c in range(part * 4, part * 4 + 4):
            weight = jnp.broadcast_to(near[:, c : c + 1], (ROWS, 128))
            total = total + weight
            for group in range(4):
                at = (group * COLS + c) * 8
                weight_ref[at : at + 8, :] = weight[group * 8 : group * 8 + 8]
        for block in range(8):
            count = total[block * 4 : block * 4 + 1]
            for k in range(1, 4):
                count = count + total[block * 4 + k : block * 4 + k + 1]
            share_ref[block * 2 + part : block * 2 + part + 1, :] = 1.0 / jnp.maximum(count, 1.0)


def filtered(tall, rim, at, rows, gain, mix):
    inner = tall[at : at + rows, :]
    beside = 0.25 * (
        tall[at + 1 : at + 1 + rows, :]
        + tall[at - 1 : at - 1 + rows, :]
        + tall[at + rim : at + rim + rows, :]
        + tall[at - rim : at - rim + rows, :]
    )
    return gain * inner + mix * (beside - inner)


def group_blocks(group, pick_ref, filt_re, filt_im, weight_ref, share_ref, out_ref, first, scratch):
    window, annulus, sums = scratch
    size = SIDE * 16
    for q in range(SIDE):
        at = q * REACH + group * 8
        for filt, lanes in ((filt_re, slice(0, FREQ)), (filt_im, slice(FREQ, 2 * FREQ))):
            value = filt[at : at + 16, :]
            high = value.astype(BF16)
            low = (value - high.astype(F32)).astype(BF16)
            window[q * 16 : q * 16 + 16, lanes] = high
            window[size + q * 16 : size + q * 16 + 16, lanes] = low
    annulus[...] = jnp.dot(pick_ref[...], window[...], preferred_element_type=F32)
    for part in range(2):
        centre = []
        for c in range(part * 4, part * 4 + 4):
            at = (c + 4) * REACH + 4 + group * 8
            weight = weight_ref[(group * COLS + c) * 8 : (group * COLS + c) * 8 + 8, :]
            centre.append((filt_re[at : at + 8, :] * weight, filt_im[at : at + 8, :] * weight))
        for d in range(DIST):
            first_sum = None
            for c in range(4):
                at = (d * COLS + part * 4 + c) * 8
                real_a = annulus[at : at + 8, :FREQ]
                imag_a = annulus[at : at + 8, FREQ:]
                real_c, imag_c = centre[c]
                one = real_c * real_a + imag_c * imag_a
                two = real_c * imag_a - imag_c * real_a
                first_sum = one if first_sum is None else first_sum + one
                second_sum = two if c == 0 else second_sum + two
            at = (part * 16 + 2 * d) * 8
            sums[at : at + 8, :] = first_sum
            sums[at + 8 : at + 16, :] = second_sum
    for half in range(2):
        for part in range(2):
            block = (group * 2 + half) * 2 + part
            share = jnp.broadcast_to(share_ref[block : block + 1, :], (8, 128))
            for piece in range(2):
                base = (part * 16 + piece * 8) * 8 + half * 4
                total = sums[pl.ds(base, 8, stride=8), :]
                for k in range(1, 4):
                    total = total + sums[pl.ds(base + k, 8, stride=8), :]
                to = first + (half * 2 + part) * 16 + piece * 8
                out_ref[to : to + 8, :] = total * share


def middle_kernel(
    own_ref,
    gain_ref,
    mix_ref,
    pick_ref,
    weight_ref,
    share_ref,
    out_ref,
    filt_re,
    filt_im,
    pair_ref,
    own_re,
    own_im,
    *scratch,
):
    own_re[...] = own_ref[:, :FREQ].astype(F32)
    own_im[...] = own_ref[:, FREQ:].astype(F32)
    gain = gain_ref[...]
    mix = mix_ref[...]
    pair_ref[0:1, :] = gain
    pair_ref[1:2, :] = mix
    for source, filt in ((own_re, filt_re), (own_im, filt_im)):
        for q in range(SIDE):
            value = filtered(source, ROWS, (q + 2) * ROWS + 1, ROWS - 2, gain, mix)
            filt[q * REACH + 5 : q * REACH + 5 + ROWS - 2, :] = value
    for n in range(2):
        group_blocks(
            1 + n, pick_ref, filt_re, filt_im, weight_ref, share_ref, out_ref, n * 64, scratch
        )


def edge_blocks(
    group, upper_ref, lower_ref, pick_ref, weight_ref, share_ref, own_re, own_im, pair_ref, out_ref, scratch
):
    tall_re, tall_im, filt_re, filt_im, *scratch = scratch
    for ref, at in ((upper_ref, 0), (lower_ref, 8)):
        value = ref[...].astype(F32).reshape(WIDE, 8, 2 * FREQ)
        for q in range(WIDE):
            tall_re[at + q * 16 : at + q * 16 + 8, :] = value[q, :, :FREQ]
            tall_im[at + q * 16 : at + q * 16 + 8, :] = value[q, :, FREQ:]
    gain = pair_ref[0:1, :]
    mix = pair_ref[1:2, :]
    edge, kept = (0, 8) if group == 0 else (32, 24)
    for tall, inside, filt in ((tall_re, own_re, filt_re), (tall_im, own_im, filt_im)):
        for q in range(SIDE):
            at = q * REACH
            value = filtered(tall, 16, (q + 2) * 16 + 4, 8, gain, mix)
            filt[at + edge : at + edge + 8, :] = value
            filt[at + kept : at + kept + 8, :] = inside[at + kept : at + kept + 8, :]
    group_blocks(group, pick_ref, filt_re, filt_im, weight_ref, share_ref, out_ref, 0, scratch)


def bottom_kernel(
    last_ref, after_ref, pick_ref, weight_ref, share_ref, own_re, own_im, pair_ref, out_ref, *scratch
):
    edge_blocks(
        3,
        last_ref,
        after_ref,
        pick_ref,
        weight_ref,
        share_ref,
        own_re,
        own_im,
        pair_ref,
        out_ref,
        scratch,
    )


def top_kernel(
    before_ref,
    first_ref,
    pick_ref,
    weight_ref,
    share_ref,
    own_re,
    own_im,
    pair_ref,
    mid_ref,
    bottom_ref,
    out_ref,
    result,
    sems,
    *scratch,
):
    copies = [
        pltpu.make_async_copy(mid_ref, out_ref.at[64:192], sems.at[0]),
        pltpu.make_async_copy(bottom_ref, out_ref.at[192:256], sems.at[1]),
        pltpu.make_async_copy(result, out_ref.at[0:64], sems.at[2]),
    ]
    copies[0].start()
    copies[1].start()
    edge_blocks(
        0,
        before_ref,
        first_ref,
        pick_ref,
        weight_ref,
        share_ref,
        own_re,
        own_im,
        pair_ref,
        result,
        scratch,
    )
    copies[2].start()
    for copy in copies:
        copy.wait()


def float_shape(rows):
    return jax.ShapeDtypeStruct((rows, FREQ), F32)


VMEM = pl.BlockSpec(memory_space=pltpu.VMEM)
SMEM = pl.BlockSpec(memory_space=pltpu.SMEM)
GROUP_SCRATCH = [
    pltpu.VMEM((2 * SIDE * 16, 2 * FREQ), BF16),
    pltpu.VMEM((DIST * COLS * 8, 2 * FREQ), F32),
    pltpu.VMEM((2 * 16 * 8, FREQ), F32),
]


def params():
    return pltpu.CompilerParams(vmem_limit_bytes=32 * 1024 * 1024)


def select(steps, mask):
    return pl.pallas_call(
        select_kernel,
        out_shape=(
            jax.ShapeDtypeStruct((DIST * COLS * 8, 2 * SIDE * 16), BF16),
            float_shape(COLS * ROWS),
            float_shape(16),
        ),
        in_specs=[SMEM, VMEM],
        compiler_params=params(),
        cost_estimate=pl.CostEstimate(flops=4_000_000, bytes_accessed=4_000_000, transcendentals=0),
    )(steps, mask)


def middle(own, gain, mix, chosen):
    return pl.pallas_call(
        middle_kernel,
        out_shape=tuple(float_shape(n) for n in (128, SIDE * REACH, SIDE * REACH, 8)),
        in_specs=[VMEM] * 6,
        scratch_shapes=[pltpu.VMEM((WIDE * ROWS, FREQ), F32)] * 2 + GROUP_SCRATCH,
        compiler_params=params(),
        cost_estimate=pl.CostEstimate(flops=6_000_000, bytes_accessed=4_000_000, transcendentals=0),
    )(own, gain, mix, *chosen)


def outer(first, last, chosen, kept):
    bands = lax.axis_size("band")
    up = [(i, i + 1) for i in range(bands - 1)]
    down = [(j, i) for i, j in up]
    after = lax.ppermute(first, "band", down)
    before = lax.ppermute(last, "band", up)
    mid, *shared = kept
    rows = [WIDE * 16] * 2 + [SIDE * REACH] * 2
    scratch = [pltpu.VMEM((n, FREQ), F32) for n in rows] + GROUP_SCRATCH
    cost = pl.CostEstimate(flops=3_000_000, bytes_accessed=3_000_000, transcendentals=0)
    bottom = pl.pallas_call(
        bottom_kernel,
        out_shape=float_shape(64),
        in_specs=[VMEM] * 8,
        scratch_shapes=scratch,
        compiler_params=params(),
        cost_estimate=cost,
    )(last, after, *chosen, *shared)
    return pl.pallas_call(
        top_kernel,
        out_shape=float_shape(8 * 2 * DIST * 2),
        in_specs=[VMEM] * 10,
        out_specs=pl.BlockSpec(memory_space=pltpu.HBM),
        scratch_shapes=[pltpu.VMEM((64, FREQ), F32), pltpu.SemaphoreType.DMA((3,))] + scratch,
        compiler_params=params(),
        cost_estimate=cost,
    )(before, first, *chosen, *shared, mid, bottom)


def on_device(frames, disk_mask, offsets, filter_gain, filter_mix):
    same_core = [[2 * chip + core for chip in range(CHIPS)] for core in range(2)]
    mine = lax.all_to_all(
        pack(frames, disk_mask),
        "tile",
        split_axis=0,
        concat_axis=0,
        axis_index_groups=same_core,
        tiled=True,
    )
    steps = ((offsets[..., 1] + 4) * 16 + offsets[..., 0] + 4).reshape(DIST * OFFS)
    gain = filter_gain.reshape(1, FREQ)
    mix = filter_mix.reshape(1, FREQ)
    chosen = select(steps, disk_mask)
    other = lax.ppermute(mine, "tile", [(i, i ^ 1) for i in range(2 * CHIPS)])
    other, chosen = lax.optimization_barrier((other, chosen))
    own, first, last = spectra(mine, other, dft_table())
    out = outer(first, last, chosen, middle(own, gain, mix, chosen))
    return out.reshape(8, 2, DIST, 2, FREQ)


def solution(mesh):
    return jax.shard_map(
        on_device,
        mesh=mesh,
        in_specs=(P("tile", "band", None), P("band", None), P(), P(), P()),
        out_specs=P("band", "tile", None, None, None),
        check_vma=False,
    )
```

```python
import math

import jax
import jax.numpy as jnp
import numpy as np
from jax import lax
from jax.experimental import pallas as pl
from jax.experimental.pallas import tpu as pltpu
from jax.sharding import PartitionSpec as P

FRAMES = 512
FREQ = 128
DIST = 8
OFFS = 8
FLO = 48
CHIPS = 32
LOCAL = 8
ROWS = 32
COLS = 8
WIDE = 20
SPAN = 28
LEAD = 6
QUADS = (0, 16, 8, 24, 32, 48, 40)
MARGIN = 5
NARROW = 18
SENT = 96
BLOCKS = 72
TALL = 48
REACH = 40
SIDE = 16

F32 = jnp.float32
BF16 = jnp.bfloat16


def dft_table():
    times = np.arange(FRAMES, dtype=np.int32).reshape(CHIPS, 2, LOCAL)
    times = times.transpose(1, 0, 2).reshape(FRAMES)
    freqs = FLO + np.arange(FREQ, dtype=np.int32)
    phases = times[:, None] * freqs[None, :] % FRAMES
    angles = phases.astype(np.float32) * np.float32(2.0 * math.pi / FRAMES)
    factor = np.float32(1.0 / math.sqrt(FRAMES))
    both = np.concatenate([np.cos(angles) * factor, -np.sin(angles) * factor], axis=1)
    return jnp.asarray(both.astype(np.float32)).astype(BF16)


def exchanged(values, groups, distance):
    upper = (groups // distance) % 2 == 1
    result = list(values)
    for n in range(4):
        if (n // distance) % 2 == 0:
            m = n + distance
            result[n] = jnp.where(upper, pltpu.roll(values[m], 32 * distance, 1), values[n])
            result[m] = jnp.where(upper, values[m], pltpu.roll(values[n], 128 - 32 * distance, 1))
    return result


def pack_kernel(
    frames_ref,
    mask_ref,
    gain_ref,
    mix_ref,
    out_ref,
    pair_ref,
    frames_vmem,
    mask_vmem,
    gain_vmem,
    mix_vmem,
    pick_ref,
    low_ref,
    high_ref,
    sems,
):
    copies = [
        pltpu.make_async_copy(mask_ref, mask_vmem, sems.at[0]),
        pltpu.make_async_copy(frames_ref, frames_vmem, sems.at[1]),
        pltpu.make_async_copy(gain_ref, gain_vmem, sems.at[2]),
        pltpu.make_async_copy(mix_ref, mix_vmem, sems.at[3]),
    ]
    for copy in copies:
        copy.start()
    width = mask_vmem.shape[1]
    cols = lax.broadcasted_iota(jnp.int32, (BLOCKS, width), 1)
    block = lax.broadcasted_iota(jnp.int32, (BLOCKS, width), 0)
    place = cols - 8 * block + LEAD
    for c in range(COLS):
        pick_ref[c * BLOCKS : (c + 1) * BLOCKS, :] = jnp.where(place == c, 1.0, 0.0)
    for copy in copies:
        copy.wait()
    pair_ref[0:1, :] = gain_vmem[...]
    pair_ref[1:2, :] = mix_vmem[...]
    mask = mask_vmem[...].astype(F32)
    masked = (frames_vmem[...].astype(F32) * mask[None]).astype(BF16)
    turned = lax.dot_general(
        pick_ref[...].astype(BF16),
        masked.reshape(LOCAL * ROWS, width),
        (((1,), (1,)), ((), ())),
        preferred_element_type=F32,
    )
    groups = lax.broadcasted_iota(jnp.int32, (BLOCKS, 128), 1) // 32
    for part, ref in ((0, low_ref), (1, high_ref)):
        for half in range(2):
            lanes = slice(half * 128, half * 128 + 128)
            values = [
                turned[(part * 4 + g) * BLOCKS : (part * 4 + g + 1) * BLOCKS, lanes]
                for g in range(4)
            ]
            values = exchanged(exchanged(values, groups, 2), groups, 1)
            for f in range(4):
                ref[pl.ds(half * 4 + f, BLOCKS, stride=LOCAL), :] = values[f]
    count = CHIPS * 16
    for at, ref, start in ((0, low_ref, 0), (16, high_ref, 0), (32, low_ref, 16)):
        laid = ref[start : start + count, :].reshape(CHIPS, 16, 128)
        out_ref[:, at : at + 16, :] = laid.astype(BF16)
    laid = high_ref[16 : 16 + count, :].reshape(CHIPS, 16, 128)
    out_ref[:, 48:56, :] = laid[:, 0:8, :].astype(BF16)


def pack(frames, mask, gain, mix):
    return pl.pallas_call(
        pack_kernel,
        out_shape=(pltpu.VMEM((CHIPS, 2 * SPAN, 128), BF16), pltpu.VMEM((8, FREQ), F32)),
        in_specs=[pl.BlockSpec(memory_space=pltpu.HBM)] * 4,
        scratch_shapes=[
            pltpu.VMEM(frames.shape, BF16),
            pltpu.VMEM(mask.shape, jnp.int32),
            pltpu.VMEM((1, FREQ), F32),
            pltpu.VMEM((1, FREQ), F32),
            pltpu.VMEM((COLS * BLOCKS, mask.shape[1]), F32),
            pltpu.VMEM((BLOCKS * LOCAL, 128), F32),
            pltpu.VMEM((BLOCKS * LOCAL, 128), F32),
            pltpu.SemaphoreType.DMA((4,)),
        ],
        compiler_params=pltpu.CompilerParams(vmem_limit_bytes=60000000),
    )(frames, mask, gain, mix)


def spectra_kernel(
    mine_ref,
    other_ref,
    table_ref,
    own_ref,
    first_ref,
    last_ref,
    first_re,
    first_im,
    last_re,
    last_im,
):
    core = lax.axis_index("tile") % 2
    count = FRAMES // 2
    spectrum = None
    for ref, at in ((mine_ref, core), (other_ref, 1 - core)):
        quads = [ref[:, row : row + 8, :].reshape(count, 128) for row in QUADS]
        series = [jnp.where(core == 0, quads[n], quads[n + 2]) for n in range(5)]
        part = lax.dot_general(
            jnp.concatenate(series, axis=1),
            table_ref[pl.ds(pl.multiple_of(at * count, count), count), :],
            (((0,), (0,)), ((), ())),
            preferred_element_type=F32,
        )
        spectrum = part if spectrum is None else spectrum + part
    own_ref[...] = spectrum.astype(BF16)
    by_column = spectrum.reshape(WIDE, ROWS, 2 * FREQ)
    for q in range(NARROW):
        first_re[q * MARGIN : q * MARGIN + 8, :] = by_column[q + 1, :8, :FREQ]
        first_im[q * MARGIN : q * MARGIN + 8, :] = by_column[q + 1, :8, FREQ:]
    for q in reversed(range(NARROW)):
        at = q * MARGIN + 5
        last_re[at : at + 8, :] = by_column[q + 1, ROWS - 8 :, :FREQ]
        last_im[at : at + 8, :] = by_column[q + 1, ROWS - 8 :, FREQ:]
    first_ref[:, :FREQ] = first_re[0:SENT, :].astype(BF16)
    first_ref[:, FREQ:] = first_im[0:SENT, :].astype(BF16)
    last_ref[:, :FREQ] = last_re[8 : 8 + SENT, :].astype(BF16)
    last_ref[:, FREQ:] = last_im[8 : 8 + SENT, :].astype(BF16)


def spectra(mine, other, table):
    edge = jax.ShapeDtypeStruct((SENT, 2 * FREQ), BF16)
    own = jax.ShapeDtypeStruct((WIDE * ROWS, 2 * FREQ), BF16)
    return pl.pallas_call(
        spectra_kernel,
        out_shape=(own, edge, edge),
        scratch_shapes=[pltpu.VMEM((SENT + 16, FREQ), F32)] * 4,
        compiler_params=params(),
    )(mine, other, table)


def select_kernel(offsets_ref, mask_ref, pick_ref, weight_ref, share_ref):
    shape = (COLS * 8, SIDE * 16)
    pixel = lax.broadcasted_iota(jnp.int32, shape, 0)
    lane = lax.broadcasted_iota(jnp.int32, shape, 1)
    apart = lane - (pixel // 8) * 16 - pixel % 8

    def distance(d, carry):
        total = jnp.zeros(shape, F32)
        for k in range(OFFS):
            total = total + jnp.where(apart == offsets_ref[d * OFFS + k], 1.0, 0.0)
        picked = total.astype(BF16)
        at = pl.multiple_of(d * COLS * 8, COLS * 8)
        pick_ref[pl.ds(at, COLS * 8), 0 : SIDE * 16] = picked
        pick_ref[pl.ds(at, COLS * 8), SIDE * 16 : 2 * SIDE * 16] = picked
        return carry

    lax.fori_loop(0, DIST, distance, 0)
    tile = lax.axis_index("tile")
    wide = pl.multiple_of((tile // 16) * 128, 128)
    near = mask_ref[:, pl.ds(wide, 128)].astype(F32)
    near = pltpu.roll(near, (128 - 8 * (tile % 16)) % 128, 1)
    for part in range(2):
        total = jnp.zeros((ROWS, 128), F32)
        for c in range(part * 4, part * 4 + 4):
            weight = jnp.broadcast_to(near[:, c : c + 1], (ROWS, 128))
            total = total + weight
            for group in range(4):
                at = (group * COLS + c) * 8
                weight_ref[at : at + 8, :] = weight[group * 8 : group * 8 + 8]
        for block in range(8):
            count = total[block * 4 : block * 4 + 1]
            for k in range(1, 4):
                count = count + total[block * 4 + k : block * 4 + k + 1]
            share_ref[block * 2 + part : block * 2 + part + 1, :] = 1.0 / jnp.maximum(count, 1.0)


def filtered(tall, rim, at, rows, gain, mix):
    inner = tall[at : at + rows, :]
    beside = 0.25 * (
        tall[at + 1 : at + 1 + rows, :]
        + tall[at - 1 : at - 1 + rows, :]
        + tall[at + rim : at + rim + rows, :]
        + tall[at - rim : at - rim + rows, :]
    )
    return gain * inner + mix * (beside - inner)


def group_blocks(group, pick_ref, filt_re, filt_im, weight_ref, share_ref, out_ref, first, scratch):
    window, annulus, sums = scratch
    size = SIDE * 16
    for q in range(SIDE):
        at = q * REACH + group * 8
        for filt, lanes in ((filt_re, slice(0, FREQ)), (filt_im, slice(FREQ, 2 * FREQ))):
            value = filt[at : at + 16, :]
            high = value.astype(BF16)
            low = (value - high.astype(F32)).astype(BF16)
            window[q * 16 : q * 16 + 16, lanes] = high
            window[size + q * 16 : size + q * 16 + 16, lanes] = low
    annulus[...] = jnp.dot(pick_ref[...], window[...], preferred_element_type=F32)
    for part in range(2):
        centre = []
        for c in range(part * 4, part * 4 + 4):
            at = (c + 4) * REACH + 4 + group * 8
            weight = weight_ref[(group * COLS + c) * 8 : (group * COLS + c) * 8 + 8, :]
            centre.append((filt_re[at : at + 8, :] * weight, filt_im[at : at + 8, :] * weight))
        for d in range(DIST):
            first_sum = None
            for c in range(4):
                at = (d * COLS + part * 4 + c) * 8
                real_a = annulus[at : at + 8, :FREQ]
                imag_a = annulus[at : at + 8, FREQ:]
                real_c, imag_c = centre[c]
                one = real_c * real_a + imag_c * imag_a
                two = real_c * imag_a - imag_c * real_a
                first_sum = one if first_sum is None else first_sum + one
                second_sum = two if c == 0 else second_sum + two
            for n, value in enumerate((first_sum, second_sum)):
                at = (part * 16 + 2 * d + n) * 8
                value = value + pltpu.roll(value, 7, 0)
                sums[at : at + 8, :] = value + pltpu.roll(value, 6, 0)
    for half in range(2):
        for part in range(2):
            block = (group * 2 + half) * 2 + part
            share = jnp.broadcast_to(share_ref[block : block + 1, :], (8, 128))
            for piece in range(2):
                base = (part * 16 + piece * 8) * 8 + half * 4
                total = sums[pl.ds(base, 8, stride=8), :]
                to = first + (half * 2 + part) * 16 + piece * 8
                out_ref[to : to + 8, :] = total * share


def middle_kernel(
    own_ref,
    pair_ref,
    pick_ref,
    weight_ref,
    share_ref,
    out_ref,
    filt_re,
    filt_im,
    own_re,
    own_im,
    *scratch,
):
    own_re[...] = own_ref[:, :FREQ].astype(F32)
    own_im[...] = own_ref[:, FREQ:].astype(F32)
    gain = pair_ref[0:1, :]
    mix = pair_ref[1:2, :]
    for source, filt in ((own_re, filt_re), (own_im, filt_im)):
        for q in range(SIDE):
            value = filtered(source, ROWS, (q + 2) * ROWS + 1, ROWS - 2, gain, mix)
            filt[q * REACH + 5 : q * REACH + 5 + ROWS - 2, :] = value
    for n in range(2):
        group_blocks(
            1 + n, pick_ref, filt_re, filt_im, weight_ref, share_ref, out_ref, n * 64, scratch
        )


def edge_blocks(
    group, came_ref, own_ref, pick_ref, weight_ref, share_ref, own_re, own_im, pair_ref, out_ref, scratch
):
    came_re, came_im, tall_re, tall_im, filt_re, filt_im, *scratch = scratch
    came_re[8 : 8 + SENT, :] = came_ref[:, :FREQ].astype(F32)
    came_im[8 : 8 + SENT, :] = came_ref[:, FREQ:].astype(F32)
    at, before, inside = (0, 3, 8) if group == 0 else (8, 0, 0)
    row = 0 if group == 0 else ROWS - 8
    for q in range(NARROW):
        to = (q + 1) * 16
        own = own_ref[(q + 1) * ROWS : (q + 2) * ROWS, :].astype(F32)[row : row + 8]
        start = 8 + q * MARGIN - before
        tall_re[to + at : to + at + 8, :] = came_re[start : start + 8, :]
        tall_im[to + at : to + at + 8, :] = came_im[start : start + 8, :]
        tall_re[to + inside : to + inside + 8, :] = own[:, :FREQ]
        tall_im[to + inside : to + inside + 8, :] = own[:, FREQ:]
    gain = pair_ref[0:1, :]
    mix = pair_ref[1:2, :]
    edge, kept = (0, 8) if group == 0 else (32, 24)
    for tall, source, filt in ((tall_re, own_re, filt_re), (tall_im, own_im, filt_im)):
        for q in range(SIDE):
            at = q * REACH
            value = filtered(tall, 16, (q + 2) * 16 + 4, 8, gain, mix)
            filt[at + edge : at + edge + 8, :] = value
            filt[at + kept : at + kept + 8, :] = source[at + kept : at + kept + 8, :]
    group_blocks(group, pick_ref, filt_re, filt_im, weight_ref, share_ref, out_ref, 0, scratch)


def bottom_kernel(
    after_ref, own_ref, pick_ref, weight_ref, share_ref, own_re, own_im, pair_ref, out_ref, *scratch
):
    edge_blocks(
        3,
        after_ref,
        own_ref,
        pick_ref,
        weight_ref,
        share_ref,
        own_re,
        own_im,
        pair_ref,
        out_ref,
        scratch,
    )


def top_kernel(
    before_ref,
    own_ref,
    pick_ref,
    weight_ref,
    share_ref,
    own_re,
    own_im,
    pair_ref,
    mid_ref,
    bottom_ref,
    out_ref,
    result,
    sems,
    *scratch,
):
    copies = [
        pltpu.make_async_copy(mid_ref, out_ref.at[64:192], sems.at[0]),
        pltpu.make_async_copy(bottom_ref, out_ref.at[192:256], sems.at[1]),
        pltpu.make_async_copy(result, out_ref.at[0:64], sems.at[2]),
    ]
    copies[0].start()
    copies[1].start()
    edge_blocks(
        0,
        before_ref,
        own_ref,
        pick_ref,
        weight_ref,
        share_ref,
        own_re,
        own_im,
        pair_ref,
        result,
        scratch,
    )
    copies[2].start()
    for copy in copies:
        copy.wait()


def float_shape(rows):
    return jax.ShapeDtypeStruct((rows, FREQ), F32)


VMEM = pl.BlockSpec(memory_space=pltpu.VMEM)
SMEM = pl.BlockSpec(memory_space=pltpu.SMEM)
GROUP_SCRATCH = [
    pltpu.VMEM((2 * SIDE * 16, 2 * FREQ), BF16),
    pltpu.VMEM((DIST * COLS * 8, 2 * FREQ), F32),
    pltpu.VMEM((2 * 16 * 8, FREQ), F32),
]


def params():
    return pltpu.CompilerParams(vmem_limit_bytes=32 * 1024 * 1024)


def select(steps, mask):
    return pl.pallas_call(
        select_kernel,
        out_shape=(
            jax.ShapeDtypeStruct((DIST * COLS * 8, 2 * SIDE * 16), BF16),
            float_shape(COLS * ROWS),
            float_shape(16),
        ),
        in_specs=[SMEM, VMEM],
        compiler_params=params(),
        cost_estimate=pl.CostEstimate(flops=4_000_000, bytes_accessed=4_000_000, transcendentals=0),
    )(steps, mask)


def middle(own, pair, chosen):
    return pl.pallas_call(
        middle_kernel,
        out_shape=tuple(float_shape(n) for n in (128, SIDE * REACH, SIDE * REACH)),
        in_specs=[VMEM] * 5,
        scratch_shapes=[pltpu.VMEM((WIDE * ROWS, FREQ), F32)] * 2 + GROUP_SCRATCH,
        compiler_params=params(),
        cost_estimate=pl.CostEstimate(flops=6_000_000, bytes_accessed=4_000_000, transcendentals=0),
    )(own, pair, *chosen)


def outer(own, first, last, pair, chosen, kept):
    bands = lax.axis_size("band")
    up = [(i, i + 1) for i in range(bands - 1)]
    down = [(j, i) for i, j in up]
    after = lax.ppermute(first, "band", down)
    before = lax.ppermute(last, "band", up)
    mid, *shared = (*kept, pair)
    rows = [SENT + 16] * 2 + [WIDE * 16] * 2 + [SIDE * REACH] * 2
    scratch = [pltpu.VMEM((n, FREQ), F32) for n in rows] + GROUP_SCRATCH
    cost = pl.CostEstimate(flops=3_000_000, bytes_accessed=3_000_000, transcendentals=0)
    bottom = pl.pallas_call(
        bottom_kernel,
        out_shape=float_shape(64),
        in_specs=[VMEM] * 8,
        scratch_shapes=scratch,
        compiler_params=params(),
        cost_estimate=cost,
    )(after, own, *chosen, *shared)
    return pl.pallas_call(
        top_kernel,
        out_shape=float_shape(8 * 2 * DIST * 2),
        in_specs=[VMEM] * 10,
        out_specs=pl.BlockSpec(memory_space=pltpu.HBM),
        scratch_shapes=[pltpu.VMEM((64, FREQ), F32), pltpu.SemaphoreType.DMA((3,))] + scratch,
        compiler_params=params(),
        cost_estimate=cost,
    )(before, own, *chosen, *shared, mid, bottom)


def on_device(frames, disk_mask, offsets, filter_gain, filter_mix):
    same_core = [[2 * chip + core for chip in range(CHIPS)] for core in range(2)]
    gain = filter_gain.reshape(1, FREQ)
    mix = filter_mix.reshape(1, FREQ)
    packed, pair = pack(frames, disk_mask, gain, mix)
    mine = lax.all_to_all(
        packed, "tile", split_axis=0, concat_axis=0, axis_index_groups=same_core, tiled=True
    )
    other = lax.ppermute(mine, "tile", [(i, i ^ 1) for i in range(2 * CHIPS)])
    steps = ((offsets[..., 1] + 4) * 16 + offsets[..., 0] + 4).reshape(DIST * OFFS)
    chosen = select(steps, disk_mask)
    other, chosen = lax.optimization_barrier((other, chosen))
    own, first, last = spectra(mine, other, dft_table())
    out = outer(own, first, last, pair, chosen, middle(own, pair, chosen))
    return out.reshape(8, 2, DIST, 2, FREQ)


def solution(mesh):
    return jax.shard_map(
        on_device,
        mesh=mesh,
        in_specs=(P("tile", "band", None), P("band", None), P(), P(), P()),
        out_specs=P("band", "tile", None, None, None),
        check_vma=False,
    )
```

```python
import math

import jax
import jax.numpy as jnp
import numpy as np
from jax import lax
from jax.experimental import pallas as pl
from jax.experimental.pallas import tpu as pltpu
from jax.sharding import PartitionSpec as P

FRAMES = 512
FREQ = 128
DIST = 8
OFFS = 8
FLO = 48
CHIPS = 32
LOCAL = 8
ROWS = 32
COLS = 8
WIDE = 20
SPAN = 28
LEAD = 6
QUADS = (0, 16, 8, 24, 32, 48, 40)
MARGIN = 5
NARROW = 18
SENT = 96
BLOCKS = 72
TALL = 48
REACH = 40
SIDE = 16

F32 = jnp.float32
BF16 = jnp.bfloat16


def dft_table():
    times = np.arange(FRAMES, dtype=np.int32).reshape(CHIPS, 2, LOCAL)
    times = times.transpose(1, 0, 2).reshape(FRAMES)
    freqs = FLO + np.arange(FREQ, dtype=np.int32)
    phases = times[:, None] * freqs[None, :] % FRAMES
    angles = phases.astype(np.float32) * np.float32(2.0 * math.pi / FRAMES)
    factor = np.float32(1.0 / math.sqrt(FRAMES))
    both = np.concatenate([np.cos(angles) * factor, -np.sin(angles) * factor], axis=1)
    return jnp.asarray(both.astype(np.float32)).astype(BF16)


def exchanged(values, groups, distance):
    upper = (groups // distance) % 2 == 1
    result = list(values)
    for n in range(4):
        if (n // distance) % 2 == 0:
            m = n + distance
            result[n] = jnp.where(upper, pltpu.roll(values[m], 32 * distance, 1), values[n])
            result[m] = jnp.where(upper, values[m], pltpu.roll(values[n], 128 - 32 * distance, 1))
    return result


def pack_kernel(
    frames_ref,
    mask_ref,
    gain_ref,
    mix_ref,
    out_ref,
    pair_ref,
    frames_vmem,
    mask_vmem,
    gain_vmem,
    mix_vmem,
    pick_ref,
    low_ref,
    high_ref,
    sems,
):
    copies = [
        pltpu.make_async_copy(mask_ref, mask_vmem, sems.at[0]),
        pltpu.make_async_copy(gain_ref, gain_vmem, sems.at[1]),
        pltpu.make_async_copy(mix_ref, mix_vmem, sems.at[2]),
    ] + [
        pltpu.make_async_copy(frames_ref.at[f], frames_vmem.at[f], sems.at[3 + f])
        for f in range(LOCAL)
    ]
    for copy in copies:
        copy.start()
    width = mask_vmem.shape[1]
    cols = lax.broadcasted_iota(jnp.int32, (COLS * BLOCKS, width), 1)
    line = lax.broadcasted_iota(jnp.int32, (COLS * BLOCKS, width), 0)
    wanted = 8 * (line % BLOCKS) + line // BLOCKS - LEAD
    pick_ref[...] = jnp.where(cols == wanted, 1.0, 0.0).astype(BF16)
    for copy in copies:
        copy.wait()
    pair_ref[0:1, :] = gain_vmem[...]
    pair_ref[1:2, :] = mix_vmem[...]
    mask = mask_vmem[...].astype(F32)
    masked = (frames_vmem[...].astype(F32) * mask[None]).astype(BF16)
    turned = lax.dot_general(
        pick_ref[...],
        masked.reshape(LOCAL * ROWS, width),
        (((1,), (1,)), ((), ())),
        preferred_element_type=F32,
    )
    groups = lax.broadcasted_iota(jnp.int32, (BLOCKS, 128), 1) // 32
    for part, ref in ((0, low_ref), (1, high_ref)):
        for half in range(2):
            lanes = slice(half * 128, half * 128 + 128)
            values = [
                turned[(part * 4 + g) * BLOCKS : (part * 4 + g + 1) * BLOCKS, lanes]
                for g in range(4)
            ]
            values = exchanged(exchanged(values, groups, 2), groups, 1)
            for f in range(4):
                ref[pl.ds(half * 4 + f, BLOCKS, stride=LOCAL), :] = values[f]
    count = CHIPS * 16
    for at, ref, start in ((0, low_ref, 0), (16, high_ref, 0), (32, low_ref, 16)):
        laid = ref[start : start + count, :].reshape(CHIPS, 16, 128)
        out_ref[:, at : at + 16, :] = laid.astype(BF16)
    laid = high_ref[16 : 16 + count, :].reshape(CHIPS, 16, 128)
    out_ref[:, 48:56, :] = laid[:, 0:8, :].astype(BF16)


def pack(frames, mask, gain, mix):
    return pl.pallas_call(
        pack_kernel,
        out_shape=(pltpu.VMEM((CHIPS, 2 * SPAN, 128), BF16), pltpu.VMEM((8, FREQ), F32)),
        in_specs=[pl.BlockSpec(memory_space=pltpu.HBM)] * 4,
        scratch_shapes=[
            pltpu.VMEM(frames.shape, BF16),
            pltpu.VMEM(mask.shape, jnp.int32),
            pltpu.VMEM((1, FREQ), F32),
            pltpu.VMEM((1, FREQ), F32),
            pltpu.VMEM((COLS * BLOCKS, mask.shape[1]), BF16),
            pltpu.VMEM((BLOCKS * LOCAL, 128), F32),
            pltpu.VMEM((BLOCKS * LOCAL, 128), F32),
            pltpu.SemaphoreType.DMA((3 + LOCAL,)),
        ],
        compiler_params=pltpu.CompilerParams(vmem_limit_bytes=60000000),
    )(frames, mask, gain, mix)


def spectra_kernel(
    mine_ref,
    other_ref,
    table_ref,
    own_ref,
    first_ref,
    last_ref,
    first_re,
    first_im,
    last_re,
    last_im,
):
    core = lax.axis_index("tile") % 2
    count = FRAMES // 2
    spectrum = None
    for ref, at in ((mine_ref, core), (other_ref, 1 - core)):
        quads = [ref[:, row : row + 8, :].reshape(count, 128) for row in QUADS]
        series = [jnp.where(core == 0, quads[n], quads[n + 2]) for n in range(5)]
        part = lax.dot_general(
            jnp.concatenate(series, axis=1),
            table_ref[pl.ds(pl.multiple_of(at * count, count), count), :],
            (((0,), (0,)), ((), ())),
            preferred_element_type=F32,
        )
        spectrum = part if spectrum is None else spectrum + part
    own_ref[...] = spectrum.astype(BF16)
    by_column = spectrum.reshape(WIDE, ROWS, 2 * FREQ)
    for q in range(NARROW):
        first_re[q * MARGIN : q * MARGIN + 8, :] = by_column[q + 1, :8, :FREQ]
        first_im[q * MARGIN : q * MARGIN + 8, :] = by_column[q + 1, :8, FREQ:]
    for q in reversed(range(NARROW)):
        at = q * MARGIN + 5
        last_re[at : at + 8, :] = by_column[q + 1, ROWS - 8 :, :FREQ]
        last_im[at : at + 8, :] = by_column[q + 1, ROWS - 8 :, FREQ:]
    first_ref[:, :FREQ] = first_re[0:SENT, :].astype(BF16)
    first_ref[:, FREQ:] = first_im[0:SENT, :].astype(BF16)
    last_ref[:, :FREQ] = last_re[8 : 8 + SENT, :].astype(BF16)
    last_ref[:, FREQ:] = last_im[8 : 8 + SENT, :].astype(BF16)


def spectra(mine, other, table):
    edge = jax.ShapeDtypeStruct((SENT, 2 * FREQ), BF16)
    own = jax.ShapeDtypeStruct((WIDE * ROWS, 2 * FREQ), BF16)
    return pl.pallas_call(
        spectra_kernel,
        out_shape=(own, edge, edge),
        scratch_shapes=[pltpu.VMEM((SENT + 16, FREQ), F32)] * 4,
        compiler_params=params(),
    )(mine, other, table)


def select_kernel(offsets_ref, mask_ref, pick_ref, weight_ref, share_ref):
    shape = (COLS * 8, SIDE * 16)
    pixel = lax.broadcasted_iota(jnp.int32, shape, 0)
    lane = lax.broadcasted_iota(jnp.int32, shape, 1)
    apart = lane - (pixel // 8) * 16 - pixel % 8

    def distance(d, carry):
        total = jnp.zeros(shape, F32)
        for k in range(OFFS):
            total = total + jnp.where(apart == offsets_ref[d * OFFS + k], 1.0, 0.0)
        picked = total.astype(BF16)
        at = pl.multiple_of(d * COLS * 8, COLS * 8)
        pick_ref[pl.ds(at, COLS * 8), 0 : SIDE * 16] = picked
        pick_ref[pl.ds(at, COLS * 8), SIDE * 16 : 2 * SIDE * 16] = picked
        return carry

    lax.fori_loop(0, DIST, distance, 0)
    tile = lax.axis_index("tile")
    wide = pl.multiple_of((tile // 16) * 128, 128)
    near = mask_ref[:, pl.ds(wide, 128)].astype(F32)
    near = pltpu.roll(near, (128 - 8 * (tile % 16)) % 128, 1)
    for part in range(2):
        total = jnp.zeros((ROWS, 128), F32)
        for c in range(part * 4, part * 4 + 4):
            weight = jnp.broadcast_to(near[:, c : c + 1], (ROWS, 128))
            total = total + weight
            for group in range(4):
                at = (group * COLS + c) * 8
                weight_ref[at : at + 8, :] = weight[group * 8 : group * 8 + 8]
        for block in range(8):
            count = total[block * 4 : block * 4 + 1]
            for k in range(1, 4):
                count = count + total[block * 4 + k : block * 4 + k + 1]
            share_ref[block * 2 + part : block * 2 + part + 1, :] = 1.0 / jnp.maximum(count, 1.0)


def filtered(tall, rim, at, rows, gain, mix):
    inner = tall[at : at + rows, :]
    beside = 0.25 * (
        tall[at + 1 : at + 1 + rows, :]
        + tall[at - 1 : at - 1 + rows, :]
        + tall[at + rim : at + rim + rows, :]
        + tall[at - rim : at - rim + rows, :]
    )
    return gain * inner + mix * (beside - inner)


def group_blocks(group, pick_ref, filt_re, filt_im, weight_ref, share_ref, out_ref, first, scratch):
    window, annulus, sums = scratch
    size = SIDE * 16
    for q in range(SIDE):
        at = q * REACH + group * 8
        for filt, lanes in ((filt_re, slice(0, FREQ)), (filt_im, slice(FREQ, 2 * FREQ))):
            value = filt[at : at + 16, :]
            high = value.astype(BF16)
            low = (value - high.astype(F32)).astype(BF16)
            window[q * 16 : q * 16 + 16, lanes] = high
            window[size + q * 16 : size + q * 16 + 16, lanes] = low
    annulus[...] = jnp.dot(pick_ref[...], window[...], preferred_element_type=F32)
    for part in range(2):
        centre = []
        for c in range(part * 4, part * 4 + 4):
            at = (c + 4) * REACH + 4 + group * 8
            weight = weight_ref[(group * COLS + c) * 8 : (group * COLS + c) * 8 + 8, :]
            centre.append((filt_re[at : at + 8, :] * weight, filt_im[at : at + 8, :] * weight))
        for d in range(DIST):
            first_sum = None
            for c in range(4):
                at = (d * COLS + part * 4 + c) * 8
                real_a = annulus[at : at + 8, :FREQ]
                imag_a = annulus[at : at + 8, FREQ:]
                real_c, imag_c = centre[c]
                one = real_c * real_a + imag_c * imag_a
                two = real_c * imag_a - imag_c * real_a
                first_sum = one if first_sum is None else first_sum + one
                second_sum = two if c == 0 else second_sum + two
            for n, value in enumerate((first_sum, second_sum)):
                at = (part * 16 + 2 * d + n) * 8
                value = value + pltpu.roll(value, 7, 0)
                sums[at : at + 8, :] = value + pltpu.roll(value, 6, 0)
    for half in range(2):
        for part in range(2):
            block = (group * 2 + half) * 2 + part
            share = jnp.broadcast_to(share_ref[block : block + 1, :], (8, 128))
            for piece in range(2):
                base = (part * 16 + piece * 8) * 8 + half * 4
                total = sums[pl.ds(base, 8, stride=8), :]
                to = first + (half * 2 + part) * 16 + piece * 8
                out_ref[to : to + 8, :] = total * share


def middle_kernel(
    own_ref,
    pair_ref,
    pick_ref,
    weight_ref,
    share_ref,
    out_ref,
    filt_re,
    filt_im,
    own_re,
    own_im,
    *scratch,
):
    own_re[...] = own_ref[:, :FREQ].astype(F32)
    own_im[...] = own_ref[:, FREQ:].astype(F32)
    gain = pair_ref[0:1, :]
    mix = pair_ref[1:2, :]
    for source, filt in ((own_re, filt_re), (own_im, filt_im)):
        for q in range(SIDE):
            value = filtered(source, ROWS, (q + 2) * ROWS + 1, ROWS - 2, gain, mix)
            filt[q * REACH + 5 : q * REACH + 5 + ROWS - 2, :] = value
    for n in range(2):
        group_blocks(
            1 + n, pick_ref, filt_re, filt_im, weight_ref, share_ref, out_ref, n * 64, scratch
        )


def edge_blocks(
    group, came_ref, own_ref, pick_ref, weight_ref, share_ref, own_re, own_im, pair_ref, out_ref, scratch
):
    came_re, came_im, tall_re, tall_im, filt_re, filt_im, *scratch = scratch
    came_re[8 : 8 + SENT, :] = came_ref[:, :FREQ].astype(F32)
    came_im[8 : 8 + SENT, :] = came_ref[:, FREQ:].astype(F32)
    at, before, inside = (0, 3, 8) if group == 0 else (8, 0, 0)
    row = 0 if group == 0 else ROWS - 8
    for q in range(NARROW):
        to = (q + 1) * 16
        own = own_ref[(q + 1) * ROWS : (q + 2) * ROWS, :].astype(F32)[row : row + 8]
        start = 8 + q * MARGIN - before
        tall_re[to + at : to + at + 8, :] = came_re[start : start + 8, :]
        tall_im[to + at : to + at + 8, :] = came_im[start : start + 8, :]
        tall_re[to + inside : to + inside + 8, :] = own[:, :FREQ]
        tall_im[to + inside : to + inside + 8, :] = own[:, FREQ:]
    gain = pair_ref[0:1, :]
    mix = pair_ref[1:2, :]
    edge, kept = (0, 8) if group == 0 else (32, 24)
    for tall, source, filt in ((tall_re, own_re, filt_re), (tall_im, own_im, filt_im)):
        for q in range(SIDE):
            at = q * REACH
            value = filtered(tall, 16, (q + 2) * 16 + 4, 8, gain, mix)
            filt[at + edge : at + edge + 8, :] = value
            filt[at + kept : at + kept + 8, :] = source[at + kept : at + kept + 8, :]
    group_blocks(group, pick_ref, filt_re, filt_im, weight_ref, share_ref, out_ref, 0, scratch)


def bottom_kernel(
    after_ref, own_ref, pick_ref, weight_ref, share_ref, own_re, own_im, pair_ref, out_ref, *scratch
):
    edge_blocks(
        3,
        after_ref,
        own_ref,
        pick_ref,
        weight_ref,
        share_ref,
        own_re,
        own_im,
        pair_ref,
        out_ref,
        scratch,
    )


def top_kernel(
    before_ref,
    own_ref,
    pick_ref,
    weight_ref,
    share_ref,
    own_re,
    own_im,
    pair_ref,
    mid_ref,
    bottom_ref,
    out_ref,
    result,
    sems,
    *scratch,
):
    copies = [
        pltpu.make_async_copy(mid_ref, out_ref.at[64:192], sems.at[0]),
        pltpu.make_async_copy(bottom_ref, out_ref.at[192:256], sems.at[1]),
        pltpu.make_async_copy(result, out_ref.at[0:64], sems.at[2]),
    ]
    copies[0].start()
    copies[1].start()
    edge_blocks(
        0,
        before_ref,
        own_ref,
        pick_ref,
        weight_ref,
        share_ref,
        own_re,
        own_im,
        pair_ref,
        result,
        scratch,
    )
    copies[2].start()
    for copy in copies:
        copy.wait()


def float_shape(rows):
    return jax.ShapeDtypeStruct((rows, FREQ), F32)


VMEM = pl.BlockSpec(memory_space=pltpu.VMEM)
SMEM = pl.BlockSpec(memory_space=pltpu.SMEM)
GROUP_SCRATCH = [
    pltpu.VMEM((2 * SIDE * 16, 2 * FREQ), BF16),
    pltpu.VMEM((DIST * COLS * 8, 2 * FREQ), F32),
    pltpu.VMEM((2 * 16 * 8, FREQ), F32),
]


def params():
    return pltpu.CompilerParams(vmem_limit_bytes=32 * 1024 * 1024)


def select(steps, mask):
    return pl.pallas_call(
        select_kernel,
        out_shape=(
            jax.ShapeDtypeStruct((DIST * COLS * 8, 2 * SIDE * 16), BF16),
            float_shape(COLS * ROWS),
            float_shape(16),
        ),
        in_specs=[SMEM, VMEM],
        compiler_params=params(),
        cost_estimate=pl.CostEstimate(flops=4_000_000, bytes_accessed=4_000_000, transcendentals=0),
    )(steps, mask)


def middle(own, pair, chosen):
    return pl.pallas_call(
        middle_kernel,
        out_shape=tuple(float_shape(n) for n in (128, SIDE * REACH, SIDE * REACH)),
        in_specs=[VMEM] * 5,
        scratch_shapes=[pltpu.VMEM((WIDE * ROWS, FREQ), F32)] * 2 + GROUP_SCRATCH,
        compiler_params=params(),
        cost_estimate=pl.CostEstimate(flops=6_000_000, bytes_accessed=4_000_000, transcendentals=0),
    )(own, pair, *chosen)


def outer(own, first, last, pair, chosen, kept):
    bands = lax.axis_size("band")
    up = [(i, i + 1) for i in range(bands - 1)]
    down = [(j, i) for i, j in up]
    after = lax.ppermute(first, "band", down)
    before = lax.ppermute(last, "band", up)
    mid, *shared = (*kept, pair)
    rows = [SENT + 16] * 2 + [WIDE * 16] * 2 + [SIDE * REACH] * 2
    scratch = [pltpu.VMEM((n, FREQ), F32) for n in rows] + GROUP_SCRATCH
    cost = pl.CostEstimate(flops=3_000_000, bytes_accessed=3_000_000, transcendentals=0)
    bottom = pl.pallas_call(
        bottom_kernel,
        out_shape=float_shape(64),
        in_specs=[VMEM] * 8,
        scratch_shapes=scratch,
        compiler_params=params(),
        cost_estimate=cost,
    )(after, own, *chosen, *shared)
    return pl.pallas_call(
        top_kernel,
        out_shape=float_shape(8 * 2 * DIST * 2),
        in_specs=[VMEM] * 10,
        out_specs=pl.BlockSpec(memory_space=pltpu.HBM),
        scratch_shapes=[pltpu.VMEM((64, FREQ), F32), pltpu.SemaphoreType.DMA((3,))] + scratch,
        compiler_params=params(),
        cost_estimate=cost,
    )(before, own, *chosen, *shared, mid, bottom)


def on_device(frames, disk_mask, offsets, filter_gain, filter_mix):
    same_core = [[2 * chip + core for chip in range(CHIPS)] for core in range(2)]
    gain = filter_gain.reshape(1, FREQ)
    mix = filter_mix.reshape(1, FREQ)
    packed, pair = pack(frames, disk_mask, gain, mix)
    mine = lax.all_to_all(
        packed, "tile", split_axis=0, concat_axis=0, axis_index_groups=same_core, tiled=True
    )
    other = lax.ppermute(mine, "tile", [(i, i ^ 1) for i in range(2 * CHIPS)])
    steps = ((offsets[..., 1] + 4) * 16 + offsets[..., 0] + 4).reshape(DIST * OFFS)
    chosen = select(steps, disk_mask)
    other, chosen = lax.optimization_barrier((other, chosen))
    own, first, last = spectra(mine, other, dft_table())
    out = outer(own, first, last, pair, chosen, middle(own, pair, chosen))
    return out.reshape(8, 2, DIST, 2, FREQ)


def solution(mesh):
    return jax.shard_map(
        on_device,
        mesh=mesh,
        in_specs=(P("tile", "band", None), P("band", None), P(), P(), P()),
        out_specs=P("band", "tile", None, None, None),
        check_vma=False,
    )
```

```python
import math

import jax
import jax.numpy as jnp
import numpy as np
from jax import lax
from jax.experimental import pallas as pl
from jax.experimental.pallas import tpu as pltpu
from jax.sharding import PartitionSpec as P

FRAMES = 512
FREQ = 128
DIST = 8
OFFS = 8
FLO = 48
CHIPS = 32
LOCAL = 8
ROWS = 32
COLS = 8
WIDE = 20
SPAN = 28
LEAD = 6
QUADS = (0, 16, 8, 24, 32, 48, 40)
MARGIN = 5
NARROW = 18
SENT = 96
BLOCKS = 72
TALL = 48
REACH = 40
SIDE = 16

F32 = jnp.float32
BF16 = jnp.bfloat16


def dft_table():
    times = np.arange(FRAMES, dtype=np.int32).reshape(CHIPS, 2, LOCAL)
    times = times.transpose(1, 0, 2).reshape(FRAMES)
    freqs = FLO + np.arange(FREQ, dtype=np.int32)
    phases = times[:, None] * freqs[None, :] % FRAMES
    angles = phases.astype(np.float32) * np.float32(2.0 * math.pi / FRAMES)
    factor = np.float32(1.0 / math.sqrt(FRAMES))
    both = np.concatenate([np.cos(angles) * factor, -np.sin(angles) * factor], axis=1)
    return jnp.asarray(both.astype(np.float32)).astype(BF16)


def exchanged(values, groups, distance):
    upper = (groups // distance) % 2 == 1
    result = list(values)
    for n in range(4):
        if (n // distance) % 2 == 0:
            m = n + distance
            result[n] = jnp.where(upper, pltpu.roll(values[m], 32 * distance, 1), values[n])
            result[m] = jnp.where(upper, values[m], pltpu.roll(values[n], 128 - 32 * distance, 1))
    return result


def pack_kernel(
    frames_ref,
    mask_ref,
    gain_ref,
    mix_ref,
    out_ref,
    pair_ref,
    frames_vmem,
    mask_vmem,
    gain_vmem,
    mix_vmem,
    pick_ref,
    low_ref,
    high_ref,
    sems,
):
    copies = [
        pltpu.make_async_copy(mask_ref, mask_vmem, sems.at[0]),
        pltpu.make_async_copy(gain_ref, gain_vmem, sems.at[1]),
        pltpu.make_async_copy(mix_ref, mix_vmem, sems.at[2]),
    ] + [
        pltpu.make_async_copy(frames_ref.at[f], frames_vmem.at[f], sems.at[3 + f])
        for f in range(LOCAL)
    ]
    for copy in copies:
        copy.start()
    width = mask_vmem.shape[1]
    cols = lax.broadcasted_iota(jnp.int32, (COLS * BLOCKS, width), 1)
    line = lax.broadcasted_iota(jnp.int32, (COLS * BLOCKS, width), 0)
    wanted = 8 * (line % BLOCKS) + line // BLOCKS - LEAD
    pick_ref[...] = jnp.where(cols == wanted, 1.0, 0.0).astype(BF16)
    for copy in copies:
        copy.wait()
    pair_ref[0:1, :] = gain_vmem[...]
    pair_ref[1:2, :] = mix_vmem[...]
    mask = mask_vmem[...].astype(F32)
    masked = (frames_vmem[...].astype(F32) * mask[None]).astype(BF16)
    turned = lax.dot_general(
        pick_ref[...],
        masked.reshape(LOCAL * ROWS, width),
        (((1,), (1,)), ((), ())),
        preferred_element_type=F32,
    )
    groups = lax.broadcasted_iota(jnp.int32, (BLOCKS, 128), 1) // 32
    for part, ref in ((0, low_ref), (1, high_ref)):
        for half in range(2):
            lanes = slice(half * 128, half * 128 + 128)
            values = [
                turned[(part * 4 + g) * BLOCKS : (part * 4 + g + 1) * BLOCKS, lanes]
                for g in range(4)
            ]
            values = exchanged(exchanged(values, groups, 2), groups, 1)
            for f in range(4):
                ref[pl.ds(half * 4 + f, BLOCKS, stride=LOCAL), :] = values[f]
    count = CHIPS * 16
    for at, ref, start in ((0, low_ref, 0), (16, high_ref, 0), (32, low_ref, 16)):
        laid = ref[start : start + count, :].reshape(CHIPS, 16, 128)
        out_ref[:, at : at + 16, :] = laid.astype(BF16)
    laid = high_ref[16 : 16 + count, :].reshape(CHIPS, 16, 128)
    out_ref[:, 48:56, :] = laid[:, 0:8, :].astype(BF16)


def pack(frames, mask, gain, mix):
    return pl.pallas_call(
        pack_kernel,
        out_shape=(pltpu.VMEM((CHIPS, 2 * SPAN, 128), BF16), pltpu.VMEM((8, FREQ), F32)),
        in_specs=[pl.BlockSpec(memory_space=pltpu.HBM)] * 4,
        scratch_shapes=[
            pltpu.VMEM(frames.shape, BF16),
            pltpu.VMEM(mask.shape, jnp.int32),
            pltpu.VMEM((1, FREQ), F32),
            pltpu.VMEM((1, FREQ), F32),
            pltpu.VMEM((COLS * BLOCKS, mask.shape[1]), BF16),
            pltpu.VMEM((BLOCKS * LOCAL, 128), F32),
            pltpu.VMEM((BLOCKS * LOCAL, 128), F32),
            pltpu.SemaphoreType.DMA((3 + LOCAL,)),
        ],
        compiler_params=pltpu.CompilerParams(vmem_limit_bytes=60000000),
    )(frames, mask, gain, mix)


def spectra_kernel(
    mine_ref,
    other_ref,
    table_ref,
    own_ref,
    first_ref,
    last_ref,
    first_re,
    first_im,
    last_re,
    last_im,
):
    core = lax.axis_index("tile") % 2
    count = FRAMES // 2
    spectrum = None
    for ref, at in ((mine_ref, core), (other_ref, 1 - core)):
        quads = [ref[:, row : row + 8, :].reshape(count, 128) for row in QUADS]
        series = [jnp.where(core == 0, quads[n], quads[n + 2]) for n in range(5)]
        part = lax.dot_general(
            jnp.concatenate(series, axis=1),
            table_ref[pl.ds(pl.multiple_of(at * count, count), count), :],
            (((0,), (0,)), ((), ())),
            preferred_element_type=F32,
        )
        spectrum = part if spectrum is None else spectrum + part
    own_ref[...] = spectrum.astype(BF16)
    by_column = spectrum.reshape(WIDE, ROWS, 2 * FREQ)
    for q in range(NARROW):
        first_re[q * MARGIN : q * MARGIN + 8, :] = by_column[q + 1, :8, :FREQ]
        first_im[q * MARGIN : q * MARGIN + 8, :] = by_column[q + 1, :8, FREQ:]
    for q in reversed(range(NARROW)):
        at = q * MARGIN + 5
        last_re[at : at + 8, :] = by_column[q + 1, ROWS - 8 :, :FREQ]
        last_im[at : at + 8, :] = by_column[q + 1, ROWS - 8 :, FREQ:]
    first_ref[:, :FREQ] = first_re[0:SENT, :].astype(BF16)
    first_ref[:, FREQ:] = first_im[0:SENT, :].astype(BF16)
    last_ref[:, :FREQ] = last_re[8 : 8 + SENT, :].astype(BF16)
    last_ref[:, FREQ:] = last_im[8 : 8 + SENT, :].astype(BF16)


def spectra(mine, other, table):
    edge = jax.ShapeDtypeStruct((SENT, 2 * FREQ), BF16)
    own = jax.ShapeDtypeStruct((WIDE * ROWS, 2 * FREQ), BF16)
    return pl.pallas_call(
        spectra_kernel,
        out_shape=(own, edge, edge),
        scratch_shapes=[pltpu.VMEM((SENT + 16, FREQ), F32)] * 4,
        compiler_params=params(),
    )(mine, other, table)


def select_kernel(offsets_ref, mask_ref, pick_ref, weight_ref, share_ref):
    shape = (COLS * 8, SIDE * 16)
    pixel = lax.broadcasted_iota(jnp.int32, shape, 0)
    lane = lax.broadcasted_iota(jnp.int32, shape, 1)
    apart = lane - (pixel // 8) * 16 - pixel % 8

    def distance(d, carry):
        total = jnp.zeros(shape, F32)
        for k in range(OFFS):
            total = total + jnp.where(apart == offsets_ref[d * OFFS + k], 1.0, 0.0)
        picked = total.astype(BF16)
        at = pl.multiple_of(d * COLS * 8, COLS * 8)
        pick_ref[pl.ds(at, COLS * 8), 0 : SIDE * 16] = picked
        pick_ref[pl.ds(at, COLS * 8), SIDE * 16 : 2 * SIDE * 16] = picked
        return carry

    lax.fori_loop(0, DIST, distance, 0)
    tile = lax.axis_index("tile")
    wide = pl.multiple_of((tile // 16) * 128, 128)
    near = mask_ref[:, pl.ds(wide, 128)].astype(F32)
    near = pltpu.roll(near, (128 - 8 * (tile % 16)) % 128, 1)
    for part in range(2):
        total = jnp.zeros((ROWS, 128), F32)
        for c in range(part * 4, part * 4 + 4):
            weight = jnp.broadcast_to(near[:, c : c + 1], (ROWS, 128))
            total = total + weight
            for group in range(4):
                at = (group * COLS + c) * 8
                weight_ref[at : at + 8, :] = weight[group * 8 : group * 8 + 8]
        for block in range(8):
            count = total[block * 4 : block * 4 + 1]
            for k in range(1, 4):
                count = count + total[block * 4 + k : block * 4 + k + 1]
            share_ref[block * 2 + part : block * 2 + part + 1, :] = 1.0 / jnp.maximum(count, 1.0)


def filtered(tall, rim, at, rows, gain, mix):
    inner = tall[at : at + rows, :]
    beside = 0.25 * (
        tall[at + 1 : at + 1 + rows, :]
        + tall[at - 1 : at - 1 + rows, :]
        + tall[at + rim : at + rim + rows, :]
        + tall[at - rim : at - rim + rows, :]
    )
    return gain * inner + mix * (beside - inner)


def group_blocks(group, pick_ref, filt_re, filt_im, weight_ref, share_ref, out_ref, first, scratch):
    window, annulus, sums = scratch
    size = SIDE * 16
    for q in range(SIDE):
        at = q * REACH + group * 8
        for filt, lanes in ((filt_re, slice(0, FREQ)), (filt_im, slice(FREQ, 2 * FREQ))):
            value = filt[at : at + 16, :]
            high = value.astype(BF16)
            low = (value - high.astype(F32)).astype(BF16)
            window[q * 16 : q * 16 + 16, lanes] = high
            window[size + q * 16 : size + q * 16 + 16, lanes] = low
    annulus[...] = jnp.dot(pick_ref[...], window[...], preferred_element_type=F32)
    for part in range(2):
        centre = []
        for c in range(part * 4, part * 4 + 4):
            at = (c + 4) * REACH + 4 + group * 8
            weight = weight_ref[(group * COLS + c) * 8 : (group * COLS + c) * 8 + 8, :]
            centre.append((filt_re[at : at + 8, :] * weight, filt_im[at : at + 8, :] * weight))
        for d in range(DIST):
            first_sum = None
            for c in range(4):
                at = (d * COLS + part * 4 + c) * 8
                real_a = annulus[at : at + 8, :FREQ]
                imag_a = annulus[at : at + 8, FREQ:]
                real_c, imag_c = centre[c]
                one = real_c * real_a + imag_c * imag_a
                two = real_c * imag_a - imag_c * real_a
                first_sum = one if first_sum is None else first_sum + one
                second_sum = two if c == 0 else second_sum + two
            for n, value in enumerate((first_sum, second_sum)):
                at = (part * 16 + 2 * d + n) * 8
                value = value + pltpu.roll(value, 7, 0)
                sums[at : at + 8, :] = value + pltpu.roll(value, 6, 0)
    for half in range(2):
        for part in range(2):
            block = (group * 2 + half) * 2 + part
            share = jnp.broadcast_to(share_ref[block : block + 1, :], (8, 128))
            for piece in range(2):
                base = (part * 16 + piece * 8) * 8 + half * 4
                total = sums[pl.ds(base, 8, stride=8), :]
                to = first + (half * 2 + part) * 16 + piece * 8
                out_ref[to : to + 8, :] = total * share


def middle_kernel(
    own_ref,
    pair_ref,
    pick_ref,
    weight_ref,
    share_ref,
    out_ref,
    filt_re,
    filt_im,
    own_re,
    own_im,
    *scratch,
):
    own_re[...] = own_ref[:, :FREQ].astype(F32)
    own_im[...] = own_ref[:, FREQ:].astype(F32)
    gain = pair_ref[0:1, :]
    mix = pair_ref[1:2, :]
    for source, filt in ((own_re, filt_re), (own_im, filt_im)):
        for q in range(SIDE):
            value = filtered(source, ROWS, (q + 2) * ROWS + 1, ROWS - 2, gain, mix)
            filt[q * REACH + 5 : q * REACH + 5 + ROWS - 2, :] = value
    for n in range(2):
        group_blocks(
            1 + n, pick_ref, filt_re, filt_im, weight_ref, share_ref, out_ref, n * 64, scratch
        )


def edge_blocks(
    group, came_ref, own_ref, pick_ref, weight_ref, share_ref, own_re, own_im, pair_ref, out_ref, scratch
):
    came_re, came_im, tall_re, tall_im, filt_re, filt_im, *scratch = scratch
    came_re[8 : 8 + SENT, :] = came_ref[:, :FREQ].astype(F32)
    came_im[8 : 8 + SENT, :] = came_ref[:, FREQ:].astype(F32)
    at, before, inside = (0, 3, 8) if group == 0 else (8, 0, 0)
    row = 0 if group == 0 else ROWS - 8
    for q in range(NARROW):
        to = (q + 1) * 16
        own = own_ref[(q + 1) * ROWS : (q + 2) * ROWS, :].astype(F32)[row : row + 8]
        start = 8 + q * MARGIN - before
        tall_re[to + at : to + at + 8, :] = came_re[start : start + 8, :]
        tall_im[to + at : to + at + 8, :] = came_im[start : start + 8, :]
        tall_re[to + inside : to + inside + 8, :] = own[:, :FREQ]
        tall_im[to + inside : to + inside + 8, :] = own[:, FREQ:]
    gain = pair_ref[0:1, :]
    mix = pair_ref[1:2, :]
    edge, kept = (0, 8) if group == 0 else (32, 24)
    for tall, source, filt in ((tall_re, own_re, filt_re), (tall_im, own_im, filt_im)):
        for q in range(SIDE):
            at = q * REACH
            value = filtered(tall, 16, (q + 2) * 16 + 4, 8, gain, mix)
            filt[at + edge : at + edge + 8, :] = value
            filt[at + kept : at + kept + 8, :] = source[at + kept : at + kept + 8, :]
    group_blocks(group, pick_ref, filt_re, filt_im, weight_ref, share_ref, out_ref, 0, scratch)


def first_edge_kernel(
    came_ref, own_ref, pick_ref, weight_ref, share_ref, own_re, own_im, pair_ref, out_ref, *scratch
):
    edge_blocks(
        0,
        came_ref,
        own_ref,
        pick_ref,
        weight_ref,
        share_ref,
        own_re,
        own_im,
        pair_ref,
        out_ref,
        scratch,
    )


def last_edge_kernel(
    came_ref,
    own_ref,
    pick_ref,
    weight_ref,
    share_ref,
    own_re,
    own_im,
    pair_ref,
    mid_ref,
    edge_ref,
    out_ref,
    result,
    sems,
    *scratch,
):
    copies = [
        pltpu.make_async_copy(mid_ref, out_ref.at[64:192], sems.at[0]),
        pltpu.make_async_copy(edge_ref, out_ref.at[0:64], sems.at[1]),
        pltpu.make_async_copy(result, out_ref.at[192:256], sems.at[2]),
    ]
    copies[0].start()
    copies[1].start()
    edge_blocks(
        3,
        came_ref,
        own_ref,
        pick_ref,
        weight_ref,
        share_ref,
        own_re,
        own_im,
        pair_ref,
        result,
        scratch,
    )
    copies[2].start()
    for copy in copies:
        copy.wait()


def float_shape(rows):
    return jax.ShapeDtypeStruct((rows, FREQ), F32)


VMEM = pl.BlockSpec(memory_space=pltpu.VMEM)
SMEM = pl.BlockSpec(memory_space=pltpu.SMEM)
GROUP_SCRATCH = [
    pltpu.VMEM((2 * SIDE * 16, 2 * FREQ), BF16),
    pltpu.VMEM((DIST * COLS * 8, 2 * FREQ), F32),
    pltpu.VMEM((2 * 16 * 8, FREQ), F32),
]


def params():
    return pltpu.CompilerParams(vmem_limit_bytes=32 * 1024 * 1024)


def select(steps, mask):
    return pl.pallas_call(
        select_kernel,
        out_shape=(
            jax.ShapeDtypeStruct((DIST * COLS * 8, 2 * SIDE * 16), BF16),
            float_shape(COLS * ROWS),
            float_shape(16),
        ),
        in_specs=[SMEM, VMEM],
        compiler_params=params(),
        cost_estimate=pl.CostEstimate(flops=4_000_000, bytes_accessed=4_000_000, transcendentals=0),
    )(steps, mask)


def middle(own, pair, chosen):
    return pl.pallas_call(
        middle_kernel,
        out_shape=tuple(float_shape(n) for n in (128, SIDE * REACH, SIDE * REACH)),
        in_specs=[VMEM] * 5,
        scratch_shapes=[pltpu.VMEM((WIDE * ROWS, FREQ), F32)] * 2 + GROUP_SCRATCH,
        compiler_params=params(),
        cost_estimate=pl.CostEstimate(flops=6_000_000, bytes_accessed=4_000_000, transcendentals=0),
    )(own, pair, *chosen)


def outer(own, first, last, pair, chosen, kept):
    bands = lax.axis_size("band")
    up = [(i, i + 1) for i in range(bands - 1)]
    down = [(j, i) for i, j in up]
    after = lax.ppermute(first, "band", down)
    before = lax.ppermute(last, "band", up)
    mid, *shared = (*kept, pair)
    rows = [SENT + 16] * 2 + [WIDE * 16] * 2 + [SIDE * REACH] * 2
    scratch = [pltpu.VMEM((n, FREQ), F32) for n in rows] + GROUP_SCRATCH
    cost = pl.CostEstimate(flops=3_000_000, bytes_accessed=3_000_000, transcendentals=0)
    top = pl.pallas_call(
        first_edge_kernel,
        out_shape=float_shape(64),
        in_specs=[VMEM] * 8,
        scratch_shapes=scratch,
        compiler_params=params(),
        cost_estimate=cost,
    )(before, own, *chosen, *shared)
    return pl.pallas_call(
        last_edge_kernel,
        out_shape=float_shape(8 * 2 * DIST * 2),
        in_specs=[VMEM] * 10,
        out_specs=pl.BlockSpec(memory_space=pltpu.HBM),
        scratch_shapes=[pltpu.VMEM((64, FREQ), F32), pltpu.SemaphoreType.DMA((3,))] + scratch,
        compiler_params=params(),
        cost_estimate=cost,
    )(after, own, *chosen, *shared, mid, top)


def on_device(frames, disk_mask, offsets, filter_gain, filter_mix):
    same_core = [[2 * chip + core for chip in range(CHIPS)] for core in range(2)]
    gain = filter_gain.reshape(1, FREQ)
    mix = filter_mix.reshape(1, FREQ)
    packed, pair = pack(frames, disk_mask, gain, mix)
    mine = lax.all_to_all(
        packed, "tile", split_axis=0, concat_axis=0, axis_index_groups=same_core, tiled=True
    )
    other = lax.ppermute(mine, "tile", [(i, i ^ 1) for i in range(2 * CHIPS)])
    steps = ((offsets[..., 1] + 4) * 16 + offsets[..., 0] + 4).reshape(DIST * OFFS)
    chosen = select(steps, disk_mask)
    other, chosen = lax.optimization_barrier((other, chosen))
    own, first, last = spectra(mine, other, dft_table())
    out = outer(own, first, last, pair, chosen, middle(own, pair, chosen))
    return out.reshape(8, 2, DIST, 2, FREQ)


def solution(mesh):
    return jax.shard_map(
        on_device,
        mesh=mesh,
        in_specs=(P("tile", "band", None), P("band", None), P(), P(), P()),
        out_specs=P("band", "tile", None, None, None),
        check_vma=False,
    )
```

```python
import math

import jax
import jax.numpy as jnp
import numpy as np
from jax import lax
from jax.experimental import pallas as pl
from jax.experimental.pallas import tpu as pltpu
from jax.sharding import PartitionSpec as P

FRAMES = 512
FREQ = 128
DIST = 8
OFFS = 8
FLO = 48
CHIPS = 32
LOCAL = 8
ROWS = 32
COLS = 8
WIDE = 20
SPAN = 28
LEAD = 6
QUADS = (0, 16, 8, 24, 32, 48, 40)
MARGIN = 5
NARROW = 18
SENT = 96
BLOCKS = 72
TALL = 48
REACH = 40
SIDE = 16

F32 = jnp.float32
BF16 = jnp.bfloat16


def dft_table():
    times = np.arange(FRAMES, dtype=np.int32).reshape(CHIPS, 2, LOCAL)
    times = times.transpose(1, 0, 2).reshape(FRAMES)
    freqs = FLO + np.arange(FREQ, dtype=np.int32)
    phases = times[:, None] * freqs[None, :] % FRAMES
    angles = phases.astype(np.float32) * np.float32(2.0 * math.pi / FRAMES)
    factor = np.float32(1.0 / math.sqrt(FRAMES))
    both = np.concatenate([np.cos(angles) * factor, -np.sin(angles) * factor], axis=1)
    return jnp.asarray(both.astype(np.float32)).astype(BF16)


def exchanged(values, groups, distance):
    upper = (groups // distance) % 2 == 1
    result = list(values)
    for n in range(4):
        if (n // distance) % 2 == 0:
            m = n + distance
            result[n] = jnp.where(upper, pltpu.roll(values[m], 32 * distance, 1), values[n])
            result[m] = jnp.where(upper, values[m], pltpu.roll(values[n], 128 - 32 * distance, 1))
    return result


def pack_kernel(
    frames_ref,
    mask_ref,
    gain_ref,
    mix_ref,
    out_ref,
    pair_ref,
    frames_vmem,
    mask_vmem,
    gain_vmem,
    mix_vmem,
    pick_ref,
    low_ref,
    high_ref,
    sems,
):
    copies = [
        pltpu.make_async_copy(mask_ref, mask_vmem, sems.at[0]),
        pltpu.make_async_copy(gain_ref, gain_vmem, sems.at[1]),
        pltpu.make_async_copy(mix_ref, mix_vmem, sems.at[2]),
    ] + [
        pltpu.make_async_copy(frames_ref.at[f], frames_vmem.at[f], sems.at[3 + f])
        for f in range(LOCAL)
    ]
    for copy in copies:
        copy.start()
    width = mask_vmem.shape[1]
    cols = lax.broadcasted_iota(jnp.int32, (COLS * BLOCKS, width), 1)
    line = lax.broadcasted_iota(jnp.int32, (COLS * BLOCKS, width), 0)
    wanted = 8 * (line % BLOCKS) + line // BLOCKS - LEAD
    pick_ref[...] = jnp.where(cols == wanted, 1.0, 0.0).astype(BF16)
    for copy in copies:
        copy.wait()
    pair_ref[0:1, :] = gain_vmem[...]
    pair_ref[1:2, :] = mix_vmem[...]
    mask = mask_vmem[...].astype(F32)
    masked = (frames_vmem[...].astype(F32) * mask[None]).astype(BF16)
    turned = lax.dot_general(
        pick_ref[...],
        masked.reshape(LOCAL * ROWS, width),
        (((1,), (1,)), ((), ())),
        preferred_element_type=F32,
    )
    groups = lax.broadcasted_iota(jnp.int32, (BLOCKS, 128), 1) // 32
    for part, ref in ((0, low_ref), (1, high_ref)):
        for half in range(2):
            lanes = slice(half * 128, half * 128 + 128)
            values = [
                turned[(part * 4 + g) * BLOCKS : (part * 4 + g + 1) * BLOCKS, lanes]
                for g in range(4)
            ]
            values = exchanged(exchanged(values, groups, 2), groups, 1)
            for f in range(4):
                ref[pl.ds(half * 4 + f, BLOCKS, stride=LOCAL), :] = values[f]
    count = CHIPS * 16
    for at, ref, start in ((0, low_ref, 0), (16, high_ref, 0), (32, low_ref, 16)):
        laid = ref[start : start + count, :].reshape(CHIPS, 16, 128)
        out_ref[:, at : at + 16, :] = laid.astype(BF16)
    laid = high_ref[16 : 16 + count, :].reshape(CHIPS, 16, 128)
    out_ref[:, 48:56, :] = laid[:, 0:8, :].astype(BF16)


def pack(frames, mask, gain, mix):
    return pl.pallas_call(
        pack_kernel,
        out_shape=(pltpu.VMEM((CHIPS, 2 * SPAN, 128), BF16), pltpu.VMEM((8, FREQ), F32)),
        in_specs=[pl.BlockSpec(memory_space=pltpu.HBM)] * 4,
        scratch_shapes=[
            pltpu.VMEM(frames.shape, BF16),
            pltpu.VMEM(mask.shape, jnp.int32),
            pltpu.VMEM((1, FREQ), F32),
            pltpu.VMEM((1, FREQ), F32),
            pltpu.VMEM((COLS * BLOCKS, mask.shape[1]), BF16),
            pltpu.VMEM((BLOCKS * LOCAL, 128), F32),
            pltpu.VMEM((BLOCKS * LOCAL, 128), F32),
            pltpu.SemaphoreType.DMA((3 + LOCAL,)),
        ],
        compiler_params=pltpu.CompilerParams(vmem_limit_bytes=60000000),
    )(frames, mask, gain, mix)


def spectra_kernel(
    mine_ref,
    other_ref,
    table_ref,
    own_ref,
    first_ref,
    last_ref,
    first_re,
    first_im,
    last_re,
    last_im,
):
    core = lax.axis_index("tile") % 2
    count = FRAMES // 2
    spectrum = None
    for ref, at in ((mine_ref, core), (other_ref, 1 - core)):
        quads = [ref[:, row : row + 8, :].reshape(count, 128) for row in QUADS]
        series = [jnp.where(core == 0, quads[n], quads[n + 2]) for n in range(5)]
        part = lax.dot_general(
            jnp.concatenate(series, axis=1),
            table_ref[pl.ds(pl.multiple_of(at * count, count), count), :],
            (((0,), (0,)), ((), ())),
            preferred_element_type=F32,
        )
        spectrum = part if spectrum is None else spectrum + part
    own_ref[...] = spectrum.astype(BF16)
    by_column = spectrum.reshape(WIDE, ROWS, 2 * FREQ)
    for q in range(NARROW):
        first_re[q * MARGIN : q * MARGIN + 8, :] = by_column[q + 1, :8, :FREQ]
        first_im[q * MARGIN : q * MARGIN + 8, :] = by_column[q + 1, :8, FREQ:]
    for q in reversed(range(NARROW)):
        at = q * MARGIN + 5
        last_re[at : at + 8, :] = by_column[q + 1, ROWS - 8 :, :FREQ]
        last_im[at : at + 8, :] = by_column[q + 1, ROWS - 8 :, FREQ:]
    first_ref[:, :FREQ] = first_re[0:SENT, :].astype(BF16)
    first_ref[:, FREQ:] = first_im[0:SENT, :].astype(BF16)
    last_ref[:, :FREQ] = last_re[8 : 8 + SENT, :].astype(BF16)
    last_ref[:, FREQ:] = last_im[8 : 8 + SENT, :].astype(BF16)


def spectra(mine, other, table):
    edge = jax.ShapeDtypeStruct((SENT, 2 * FREQ), BF16)
    own = jax.ShapeDtypeStruct((WIDE * ROWS, 2 * FREQ), BF16)
    return pl.pallas_call(
        spectra_kernel,
        out_shape=(own, edge, edge),
        scratch_shapes=[pltpu.VMEM((SENT + 16, FREQ), F32)] * 4,
        compiler_params=params(),
    )(mine, other, table)


def select_kernel(offsets_ref, mask_ref, pick_ref, weight_ref, share_ref):
    shape = (COLS * 8, SIDE * 16)
    pixel = lax.broadcasted_iota(jnp.int32, shape, 0)
    lane = lax.broadcasted_iota(jnp.int32, shape, 1)
    apart = lane - (pixel // 8) * 16 - pixel % 8

    def distance(d, carry):
        total = jnp.zeros(shape, F32)
        for k in range(OFFS):
            total = total + jnp.where(apart == offsets_ref[d * OFFS + k], 1.0, 0.0)
        picked = total.astype(BF16)
        at = pl.multiple_of(d * COLS * 8, COLS * 8)
        pick_ref[pl.ds(at, COLS * 8), 0 : SIDE * 16] = picked
        pick_ref[pl.ds(at, COLS * 8), SIDE * 16 : 2 * SIDE * 16] = picked
        return carry

    lax.fori_loop(0, DIST, distance, 0)
    tile = lax.axis_index("tile")
    wide = pl.multiple_of((tile // 16) * 128, 128)
    near = mask_ref[:, pl.ds(wide, 128)].astype(F32)
    near = pltpu.roll(near, (128 - 8 * (tile % 16)) % 128, 1)
    for part in range(2):
        total = jnp.zeros((ROWS, 128), F32)
        for c in range(part * 4, part * 4 + 4):
            weight = jnp.broadcast_to(near[:, c : c + 1], (ROWS, 128))
            total = total + weight
            for group in range(4):
                at = (group * COLS + c) * 8
                weight_ref[at : at + 8, :] = weight[group * 8 : group * 8 + 8]
        for block in range(8):
            count = total[block * 4 : block * 4 + 1]
            for k in range(1, 4):
                count = count + total[block * 4 + k : block * 4 + k + 1]
            share_ref[block * 2 + part : block * 2 + part + 1, :] = 1.0 / jnp.maximum(count, 1.0)


def filtered(tall, rim, at, rows, gain, mix):
    inner = tall[at : at + rows, :]
    beside = 0.25 * (
        tall[at + 1 : at + 1 + rows, :]
        + tall[at - 1 : at - 1 + rows, :]
        + tall[at + rim : at + rim + rows, :]
        + tall[at - rim : at - rim + rows, :]
    )
    return gain * inner + mix * (beside - inner)


def group_blocks(group, pick_ref, filt_re, filt_im, weight_ref, share_ref, out_ref, first, scratch):
    window, annulus, sums = scratch
    size = SIDE * 16
    for q in range(SIDE):
        at = q * REACH + group * 8
        for filt, lanes in ((filt_re, slice(0, FREQ)), (filt_im, slice(FREQ, 2 * FREQ))):
            value = filt[at : at + 16, :]
            high = value.astype(BF16)
            low = (value - high.astype(F32)).astype(BF16)
            window[q * 16 : q * 16 + 16, lanes] = high
            window[size + q * 16 : size + q * 16 + 16, lanes] = low
    annulus[...] = jnp.dot(pick_ref[...], window[...], preferred_element_type=F32)
    for part in range(2):
        centre = []
        for c in range(part * 4, part * 4 + 4):
            at = (c + 4) * REACH + 4 + group * 8
            weight = weight_ref[(group * COLS + c) * 8 : (group * COLS + c) * 8 + 8, :]
            centre.append((filt_re[at : at + 8, :] * weight, filt_im[at : at + 8, :] * weight))
        for d in range(DIST):
            first_sum = None
            for c in range(4):
                at = (d * COLS + part * 4 + c) * 8
                real_a = annulus[at : at + 8, :FREQ]
                imag_a = annulus[at : at + 8, FREQ:]
                real_c, imag_c = centre[c]
                one = real_c * real_a + imag_c * imag_a
                two = real_c * imag_a - imag_c * real_a
                first_sum = one if first_sum is None else first_sum + one
                second_sum = two if c == 0 else second_sum + two
            for n, value in enumerate((first_sum, second_sum)):
                at = (part * 16 + 2 * d + n) * 8
                value = value + pltpu.roll(value, 7, 0)
                sums[at : at + 8, :] = value + pltpu.roll(value, 6, 0)
    for half in range(2):
        for part in range(2):
            block = (group * 2 + half) * 2 + part
            share = jnp.broadcast_to(share_ref[block : block + 1, :], (8, 128))
            for piece in range(2):
                base = (part * 16 + piece * 8) * 8 + half * 4
                total = sums[pl.ds(base, 8, stride=8), :]
                to = first + (half * 2 + part) * 16 + piece * 8
                out_ref[to : to + 8, :] = total * share


def middle_kernel(
    own_ref,
    pair_ref,
    pick_ref,
    weight_ref,
    share_ref,
    out_ref,
    filt_re,
    filt_im,
    own_re,
    own_im,
    *scratch,
):
    own_re[...] = own_ref[:, :FREQ].astype(F32)
    own_im[...] = own_ref[:, FREQ:].astype(F32)
    gain = pair_ref[0:1, :]
    mix = pair_ref[1:2, :]
    for source, filt in ((own_re, filt_re), (own_im, filt_im)):
        for q in range(SIDE):
            value = filtered(source, ROWS, (q + 2) * ROWS + 1, ROWS - 2, gain, mix)
            filt[q * REACH + 5 : q * REACH + 5 + ROWS - 2, :] = value
    for n in range(2):
        group_blocks(
            1 + n, pick_ref, filt_re, filt_im, weight_ref, share_ref, out_ref, n * 64, scratch
        )


def edge_blocks(
    group, came_ref, own_ref, pick_ref, weight_ref, share_ref, own_re, own_im, pair_ref, out_ref, scratch
):
    came_re, came_im, tall_re, tall_im, filt_re, filt_im, *scratch = scratch
    came_re[8 : 8 + SENT, :] = came_ref[:, :FREQ].astype(F32)
    came_im[8 : 8 + SENT, :] = came_ref[:, FREQ:].astype(F32)
    at, before, inside = (0, 3, 8) if group == 0 else (8, 0, 0)
    row = 0 if group == 0 else ROWS - 8
    for q in range(NARROW):
        to = (q + 1) * 16
        own = own_ref[(q + 1) * ROWS : (q + 2) * ROWS, :].astype(F32)[row : row + 8]
        start = 8 + q * MARGIN - before
        tall_re[to + at : to + at + 8, :] = came_re[start : start + 8, :]
        tall_im[to + at : to + at + 8, :] = came_im[start : start + 8, :]
        tall_re[to + inside : to + inside + 8, :] = own[:, :FREQ]
        tall_im[to + inside : to + inside + 8, :] = own[:, FREQ:]
    gain = pair_ref[0:1, :]
    mix = pair_ref[1:2, :]
    edge, kept = (0, 8) if group == 0 else (32, 24)
    for tall, source, filt in ((tall_re, own_re, filt_re), (tall_im, own_im, filt_im)):
        for q in range(SIDE):
            at = q * REACH
            value = filtered(tall, 16, (q + 2) * 16 + 4, 8, gain, mix)
            filt[at + edge : at + edge + 8, :] = value
            filt[at + kept : at + kept + 8, :] = source[at + kept : at + kept + 8, :]
    group_blocks(group, pick_ref, filt_re, filt_im, weight_ref, share_ref, out_ref, 0, scratch)


def bottom_kernel(
    after_ref, own_ref, pick_ref, weight_ref, share_ref, own_re, own_im, pair_ref, out_ref, *scratch
):
    edge_blocks(
        3,
        after_ref,
        own_ref,
        pick_ref,
        weight_ref,
        share_ref,
        own_re,
        own_im,
        pair_ref,
        out_ref,
        scratch,
    )


def top_kernel(
    before_ref,
    own_ref,
    pick_ref,
    weight_ref,
    share_ref,
    own_re,
    own_im,
    pair_ref,
    mid_ref,
    bottom_ref,
    out_ref,
    result,
    sems,
    *scratch,
):
    copies = [
        pltpu.make_async_copy(mid_ref, out_ref.at[64:192], sems.at[0]),
        pltpu.make_async_copy(bottom_ref, out_ref.at[192:256], sems.at[1]),
        pltpu.make_async_copy(result, out_ref.at[0:64], sems.at[2]),
    ]
    copies[0].start()
    copies[1].start()
    edge_blocks(
        0,
        before_ref,
        own_ref,
        pick_ref,
        weight_ref,
        share_ref,
        own_re,
        own_im,
        pair_ref,
        result,
        scratch,
    )
    copies[2].start()
    for copy in copies:
        copy.wait()


def float_shape(rows):
    return jax.ShapeDtypeStruct((rows, FREQ), F32)


VMEM = pl.BlockSpec(memory_space=pltpu.VMEM)
SMEM = pl.BlockSpec(memory_space=pltpu.SMEM)
GROUP_SCRATCH = [
    pltpu.VMEM((2 * SIDE * 16, 2 * FREQ), BF16),
    pltpu.VMEM((DIST * COLS * 8, 2 * FREQ), F32),
    pltpu.VMEM((2 * 16 * 8, FREQ), F32),
]


def params():
    return pltpu.CompilerParams(vmem_limit_bytes=32 * 1024 * 1024)


def select(steps, mask):
    return pl.pallas_call(
        select_kernel,
        out_shape=(
            jax.ShapeDtypeStruct((DIST * COLS * 8, 2 * SIDE * 16), BF16),
            float_shape(COLS * ROWS),
            float_shape(16),
        ),
        in_specs=[SMEM, VMEM],
        compiler_params=params(),
        cost_estimate=pl.CostEstimate(flops=4_000_000, bytes_accessed=4_000_000, transcendentals=0),
    )(steps, mask)


def middle(own, pair, chosen):
    return pl.pallas_call(
        middle_kernel,
        out_shape=tuple(float_shape(n) for n in (128, SIDE * REACH, SIDE * REACH)),
        in_specs=[VMEM] * 5,
        scratch_shapes=[pltpu.VMEM((WIDE * ROWS, FREQ), F32)] * 2 + GROUP_SCRATCH,
        compiler_params=params(),
        cost_estimate=pl.CostEstimate(flops=6_000_000, bytes_accessed=4_000_000, transcendentals=0),
    )(own, pair, *chosen)


def outer(own, first, last, pair, chosen, kept):
    bands = lax.axis_size("band")
    up = [(i, i + 1) for i in range(bands - 1)]
    down = [(j, i) for i, j in up]
    after = lax.ppermute(first, "band", down)
    before = lax.ppermute(last, "band", up)
    mid, *shared = (*kept, pair)
    rows = [SENT + 16] * 2 + [WIDE * 16] * 2 + [SIDE * REACH] * 2
    scratch = [pltpu.VMEM((n, FREQ), F32) for n in rows] + GROUP_SCRATCH
    cost = pl.CostEstimate(flops=3_000_000, bytes_accessed=3_000_000, transcendentals=0)
    bottom = pl.pallas_call(
        bottom_kernel,
        out_shape=float_shape(64),
        in_specs=[VMEM] * 8,
        scratch_shapes=scratch,
        compiler_params=params(),
        cost_estimate=cost,
    )(after, own, *chosen, *shared)
    return pl.pallas_call(
        top_kernel,
        out_shape=float_shape(8 * 2 * DIST * 2),
        in_specs=[VMEM] * 10,
        out_specs=pl.BlockSpec(memory_space=pltpu.HBM),
        scratch_shapes=[pltpu.VMEM((64, FREQ), F32), pltpu.SemaphoreType.DMA((3,))] + scratch,
        compiler_params=params(),
        cost_estimate=cost,
    )(before, own, *chosen, *shared, mid, bottom)


def on_device(frames, disk_mask, offsets, filter_gain, filter_mix):
    same_core = [[2 * chip + core for chip in range(CHIPS)] for core in range(2)]
    gain = filter_gain.reshape(1, FREQ)
    mix = filter_mix.reshape(1, FREQ)
    packed, pair = pack(frames, disk_mask, gain, mix)
    mine = lax.all_to_all(
        packed, "tile", split_axis=0, concat_axis=0, axis_index_groups=same_core, tiled=True
    )
    other = lax.ppermute(mine, "tile", [(i, i ^ 1) for i in range(2 * CHIPS)])
    steps = ((offsets[..., 1] + 4) * 16 + offsets[..., 0] + 4).reshape(DIST * OFFS)
    chosen = select(steps, disk_mask)
    own, first, last = spectra(mine, other, dft_table())
    out = outer(own, first, last, pair, chosen, middle(own, pair, chosen))
    return out.reshape(8, 2, DIST, 2, FREQ)


def solution(mesh):
    return jax.shard_map(
        on_device,
        mesh=mesh,
        in_specs=(P("tile", "band", None), P("band", None), P(), P(), P()),
        out_specs=P("band", "tile", None, None, None),
        check_vma=False,
    )
```
